256 devices in a mesh: row: 8 (over y_lo, x), col: 32 (over y_hi, z, core).
Axes of the slice: x: 4, y: 4 (y_hi: 2, y_lo: 2; y = y_hi * 2 + y_lo), z: 8, core: 2. Of those that a mesh axis runs over, the one named last changes fastest.
Arguments:
- features: bfloat16 [64, 65536], P(None, ('col', 'row')), may hold values from -4.5 to 4.5
- groups: int32 [65536], P(('col', 'row')), may hold values from 0 to 7
- targets: float32 [32, 65536], P(None, ('col', 'row')), may hold values from -7.5 to 7.5
- start: float32 [32, 65536], P(None, ('col', 'row')), may hold values from -3 to 3
Outputs:
- solution: float32 [32, 65536], P(None, ('col', 'row'))
- residual: float32 [32, 65536], P(None, ('col', 'row'))
- direction: float32 [32, 65536], P(None, ('col', 'row'))
The draws below stay inside these ranges and needn't reach their ends.
All inputs are finite; a program needn't handle non-finite values.
Results may differ from the reference program's by a relative error of at most 0.0032.
Values may be sent and summed in bfloat16 or wider, within the bound.
No kernel may reach another device: no remote copies, remote signals or barrier semaphores. Data moves between devices by JAX's collectives and lax.ppermute only.
A program may use at most 64 MiB of HBM per device.

```python
import math
import jax
import jax.numpy as jnp
from jax import lax

F = 64
R = 32
GROUPS = 8
NPTS = 65536


manifold_dims = 4


def draw_targets(key, part):
    key = jax.random.fold_in(key, 7)
    scale_key, value_key = jax.random.split(key)
    scales = jnp.exp(jax.random.uniform(scale_key, (1, NPTS), jnp.float32, 0.0, math.log(10.0)))
    values = jax.random.truncated_normal(value_key, -3.0, 3.0, (R, NPTS), jnp.float32)
    return values * scales * 0.25


def draw_features(key, part):
    key = jax.random.fold_in(key, 11)
    coord_key, sign_key, noise_key = jax.random.split(key, 3)
    reach = 1.5 * math.sqrt(F)
    coords = jax.random.uniform(coord_key, (manifold_dims, NPTS), jnp.float32, -reach, reach)
    noise = 0.5 * jax.random.truncated_normal(noise_key, -3.0, 3.0, (F, NPTS), jnp.float32)
    signs = 2.0 * jax.random.bernoulli(sign_key, 0.5, (F,)).astype(jnp.float32) - 1.0
    owner = jnp.arange(F) % manifold_dims
    weights = signs / math.sqrt(F / manifold_dims)
    return (coords[owner, :] * weights[:, None] + noise).astype(jnp.bfloat16)


def plant(array, rng, least, high):
    dims = array.shape
    place = [jax.random.randint(jax.random.fold_in(rng, axis), (), 0, dims[axis]) for axis in range(len(dims))]
    array = array.at[tuple(place)].set(least)
    longest = dims.index(max(dims))
    place[longest] = (place[longest] + 1) % dims[longest]
    return array.at[tuple(place)].set(high)


def levels(rng, extent, cuts, low, largest):
    def one(axis_at, parts):
        steps = jax.random.uniform(jax.random.fold_in(jax.random.fold_in(rng, 6), axis_at), (parts,), jnp.float32, low / len(cuts), largest / len(cuts))
        return jnp.repeat(jnp.exp(steps), extent[axis_at] // parts).reshape((-1,) + (1,) * (len(extent) - axis_at - 1))

    loudness = one(*cuts[0])
    for cut in cuts[1:]:
        loudness = loudness * one(*cut)
    return loudness


def normal_values(own_key, shape, spread, most, cuts=(), dtype=jnp.bfloat16):
    result = jax.random.normal(own_key, shape, jnp.float32) * spread
    if len(cuts) > 0:
        result = levels(own_key, shape, cuts, -0.22, 0.18) * result
    return jnp.clip(result, min=-most, max=most).astype(dtype)


def setup_inputs(seed: int = 0) -> dict:
    seeds = jax.random.split(jax.random.key(seed), 5)
    return {
        "features": draw_features(jax.random.fold_in(seeds[4], 71), 0),
        "groups": plant(jax.random.randint(seeds[1], (NPTS,), 0, GROUPS), jax.random.fold_in(seeds[1], 1), 0, GROUPS - 1).astype(jnp.int32),
        "targets": draw_targets(jax.random.fold_in(seeds[4], 71), 0),
        "start": normal_values(seeds[3], (R, NPTS), 0.5, 3.0, ((1, 256),), jnp.float32),
    }


RHO = 0.2
NOISE = 1.0
AMP_NUM = 16.0

def apply_operator(vector, features, groups):
    width = features.shape[0]
    npoints = features.shape[1]
    amplitude = AMP_NUM / math.sqrt(npoints)
    wide = features.astype(jnp.float32)
    squares = lax.optimization_barrier(jnp.sum(wide * wide, axis=0))
    rounded = lax.optimization_barrier(vector.astype(jnp.bfloat16)).astype(jnp.float32)
    block_size = min(512, npoints)

    def one_block(first):
        rows = lax.dynamic_slice_in_dim(wide, first, block_size, 1)
        row_squares = lax.dynamic_slice_in_dim(squares, first, block_size, 0)
        row_groups = lax.dynamic_slice_in_dim(groups, first, block_size, 0)
        cross = jnp.dot(rows.T, wide, precision=lax.Precision.HIGHEST)
        distance = row_squares[:, None] + squares[None, :] - 2.0 * cross
        same = (row_groups[:, None] == groups[None, :]).astype(jnp.float32)
        tile = amplitude * jnp.exp(-distance / width) * (RHO + (1.0 - RHO) * same)
        tile = lax.optimization_barrier(tile.astype(jnp.bfloat16)).astype(jnp.float32)
        return jnp.dot(rounded, tile.T, precision=lax.Precision.HIGHEST)
    firsts = (jnp.arange(npoints // block_size) * block_size).astype(jnp.int32)
    blocks = lax.map(one_block, firsts)
    product = jnp.transpose(blocks, (1, 0, 2)).reshape(vector.shape)
    return NOISE * vector + product

def reference(features, groups, targets, start):
    residual0 = targets - apply_operator(start, features, groups)
    norm_old = lax.optimization_barrier(jnp.sum(residual0 * residual0, axis=1))
    image = apply_operator(residual0, features, groups)
    alpha = norm_old / lax.optimization_barrier(jnp.sum(residual0 * image, axis=1))
    solution = start + alpha[:, None] * residual0
    residual = residual0 - alpha[:, None] * image
    norm_new = lax.optimization_barrier(jnp.sum(residual * residual, axis=1))
    direction = residual + (norm_new / norm_old)[:, None] * residual0
    return (solution, residual, direction)
```

```python
import functools
import math

import jax
import jax.numpy as jnp
from jax import lax
from jax.experimental import pallas as pl
from jax.experimental.pallas import tpu as pltpu
from jax.sharding import Mesh, PartitionSpec as P

RHO = 0.2
AMP_NUM = 16.0

AXES = ("yl", "x", "yh", "z", "core")
PLANE = ("yl", "x", "yh")
LINE = ("z",)

BF16 = jnp.bfloat16
F32 = jnp.float32

HEAD = 80
DEPTH = 128
WIDE = 512


def scale_of(width):
    return 2.0 * math.log2(math.e) / width


def pieces_of(value):
    first = value.astype(BF16).astype(F32)
    rest = value - first
    second = rest.astype(BF16).astype(F32)
    return first, second, rest - second


def constant_pieces(value):
    import numpy as np
    import ml_dtypes

    out = []
    rest = value
    for _ in range(3):
        piece = float(np.float32(rest).astype(ml_dtypes.bfloat16))
        out.append(piece)
        rest = rest - piece
    return out


def pack_body(features_ref, groups_ref, start_ref, plane_ref, line_ref, *, shift):
    features = features_ref[...]
    wide = features.astype(F32)
    half = shift - 0.5 * jnp.sum(wide * wide, axis=0, keepdims=True)
    first, second, third = pieces_of(half)
    group = groups_ref[...].astype(F32)
    count = features.shape[1]
    row = lax.broadcasted_iota(jnp.int32, (16, count), 0)
    tail = jnp.where(row == 0, first, 0.0)
    tail = jnp.where(row == 1, second, tail)
    tail = jnp.where(row == 2, third, tail)
    tail = jnp.where(row == 3, group, tail).astype(BF16)
    vector = start_ref[...].astype(BF16)
    for n in range(plane_ref.shape[0]):
        plane_ref[n, 0:64, :] = features
        plane_ref[n, 64:80, :] = tail
    for n in range(line_ref.shape[0]):
        line_ref[n, 0:64, :] = features
        line_ref[n, 64:80, :] = tail
        line_ref[n, 80:112, :] = vector


def tail_rows(packed, left, gains):
    count = packed.shape[1]
    head = packed.astype(F32)
    first, second, third, group = (head[n : n + 1, :] for n in range(4))
    row = lax.broadcasted_iota(jnp.int32, (64, count), 0)
    level = (row & 7).astype(F32)
    hot = jnp.where(level == group, 1.0, 0.0)
    if not left:
        hot = hot * jnp.where(row < 16, gains[0], jnp.where(row < 24, gains[1], gains[2]))
    out = jnp.where((row >= 8) & (row < 32), hot, 0.0)
    base = 0 if left else 3
    out = jnp.where((row >= 3 - base) & (row < 6 - base), 1.0, out)
    out = jnp.where(row == base, first, out)
    out = jnp.where(row == base + 1, second, out)
    out = jnp.where(row == base + 2, third, out)
    return out.astype(BF16)


def build_body(scale, gains, added, line_ref, plane_ref, *refs):
    if added:
        carried_ref, tile_ref, out_ref, left_ref, vector_ref, right_ref = refs
    else:
        tile_ref, out_ref, left_ref, vector_ref, right_ref = refs
    blocks, _, size = line_ref.shape

    @pl.when(pl.program_id(0) == 0)
    def _():
        for n in range(blocks):
            rows = line_ref[n, 0:64, :]
            tail = tail_rows(line_ref[n, 64:80, :], True, gains)
            left_ref[n * size : (n + 1) * size, :] = jnp.concatenate([rows, tail], axis=0).T
            vector_ref[:, n * size : (n + 1) * size] = line_ref[n, 80:112, :]

    for n in range(plane_ref.shape[0]):
        right_ref[0:64, n * size : (n + 1) * size] = plane_ref[n, 0:64, :]
        right_ref[64:128, n * size : (n + 1) * size] = tail_rows(
            plane_ref[n, 64:80, :], False, gains
        )
    right = right_ref[...]
    for n in range(blocks):
        power = jnp.dot(
            left_ref[n * size : (n + 1) * size, :], right, preferred_element_type=F32
        )
        tile_ref[n * size : (n + 1) * size, :] = jnp.exp2(power * scale).astype(BF16)
    product = jnp.dot(vector_ref[...], tile_ref[...], preferred_element_type=F32)
    for n in range(plane_ref.shape[0]):
        value = product[:, n * size : (n + 1) * size]
        if added:
            value = value + carried_ref[n]
        out_ref[n] = value.astype(out_ref.dtype)


def build(line, plane, carried, scale, gains, out_dtype):
    blocks, rows, size = line.shape
    columns = plane.shape[0]
    per = WIDE // size
    vectors = rows - HEAD
    points = blocks * size
    in_specs = [
        pl.BlockSpec(line.shape, lambda j: (0, 0, 0)),
        pl.BlockSpec((per, HEAD, size), lambda j: (j, 0, 0)),
    ]
    operands = [line, plane]
    if carried is not None:
        in_specs.append(pl.BlockSpec((per, vectors, size), lambda j: (j, 0, 0)))
        operands.append(carried)
    return pl.pallas_call(
        functools.partial(build_body, scale, gains, carried is not None),
        grid=(columns // per,),
        in_specs=in_specs,
        out_specs=[
            pl.BlockSpec((points, WIDE), lambda j: (0, j)),
            pl.BlockSpec((per, vectors, size), lambda j: (j, 0, 0)),
        ],
        out_shape=[
            jax.ShapeDtypeStruct((points, columns * size), BF16),
            jax.ShapeDtypeStruct((columns, vectors, size), out_dtype),
        ],
        scratch_shapes=[
            pltpu.VMEM((points, DEPTH), BF16),
            pltpu.VMEM((vectors, points), BF16),
            pltpu.VMEM((DEPTH, WIDE), BF16),
        ],
        compiler_params=pltpu.CompilerParams(vmem_limit_bytes=40 << 20),
        cost_estimate=pl.CostEstimate(
            flops=2 * points * columns * size * 512,
            bytes_accessed=2 * points * columns * size,
            transcendentals=points * columns * size,
        ),
        name="build",
    )(*operands)


def apply_body(added, vector_ref, tile_ref, *refs):
    if added:
        carried_ref, out_ref, flat_ref = refs
    else:
        out_ref, flat_ref = refs
    blocks, _, size = vector_ref.shape

    @pl.when(pl.program_id(0) == 0)
    def _():
        for n in range(blocks):
            flat_ref[:, n * size : (n + 1) * size] = vector_ref[n]

    product = jnp.dot(flat_ref[...], tile_ref[...], preferred_element_type=F32)
    for n in range(out_ref.shape[0]):
        value = product[:, n * size : (n + 1) * size]
        if added:
            value = value + carried_ref[n]
        out_ref[n] = value.astype(out_ref.dtype)


def apply(vector, tile, carried, out_dtype):
    blocks, vectors, size = vector.shape
    points, total = tile.shape
    per = WIDE // size
    in_specs = [
        pl.BlockSpec(vector.shape, lambda j: (0, 0, 0)),
        pl.BlockSpec((points, WIDE), lambda j: (0, j)),
    ]
    operands = [vector, tile]
    if carried is not None:
        in_specs.append(pl.BlockSpec((per, vectors, size), lambda j: (j, 0, 0)))
        operands.append(carried)
    return pl.pallas_call(
        functools.partial(apply_body, carried is not None),
        grid=(total // WIDE,),
        in_specs=in_specs,
        out_specs=pl.BlockSpec((per, vectors, size), lambda j: (j, 0, 0)),
        out_shape=jax.ShapeDtypeStruct((total // size, vectors, size), out_dtype),
        scratch_shapes=[pltpu.VMEM((vectors, points), BF16)],
        compiler_params=pltpu.CompilerParams(vmem_limit_bytes=40 << 20),
        cost_estimate=pl.CostEstimate(
            flops=2 * points * total * 256,
            bytes_accessed=2 * points * total,
            transcendentals=0,
        ),
        name="apply",
    )(*operands)


def first_body(received_ref, targets_ref, start_ref, residual_ref, line_ref):
    product = jnp.sum(received_ref[...].astype(F32), axis=0)
    residual = targets_ref[...] - (start_ref[...] + product)
    residual_ref[...] = residual
    rounded = residual.astype(BF16)
    for n in range(line_ref.shape[0]):
        line_ref[n] = rounded


def sums_body(received_ref, residual_ref, product_ref, sums_ref):
    product = jnp.sum(received_ref[...].astype(F32), axis=0)
    product_ref[...] = product
    residual = residual_ref[...]
    vectors = residual.shape[0]
    one = jnp.sum(residual * residual, axis=1, keepdims=True)
    two = jnp.sum(residual * product, axis=1, keepdims=True)
    three = jnp.sum(product * product, axis=1, keepdims=True)
    lane = lax.broadcasted_iota(jnp.int32, (vectors, 128), 1)
    table = jnp.where(lane == 0, one, jnp.where(lane == 1, two, jnp.where(lane == 2, three, 0.0)))
    table = jnp.concatenate([table, jnp.zeros((128 - vectors, 128), F32)], axis=0).T[0:8, :]
    for n in range(sums_ref.shape[0]):
        sums_ref[n] = table


def spread_body(received_ref, sums_ref):
    table = jnp.sum(received_ref[...], axis=0)
    for n in range(sums_ref.shape[0]):
        sums_ref[n] = table


def total_body(received_ref, sums_ref):
    sums_ref[...] = jnp.sum(received_ref[...], axis=0)


def last_body(
    mine_ref, other_ref, start_ref, residual_ref, product_ref, solution_ref, new_ref, direction_ref
):
    vectors = start_ref.shape[0]
    table = mine_ref[...] + other_ref[...]
    table = jnp.concatenate([table, jnp.zeros((120, 128), F32)], axis=0).T[0:vectors, :]
    one, two, three = table[:, 0:1], table[:, 1:2], table[:, 2:3]
    alpha = one / (one + two)
    norm_new = alpha * alpha * jnp.maximum(three - two * two / one, 0.0)
    residual = residual_ref[...]
    image = residual + product_ref[...]
    solution_ref[...] = start_ref[...] + alpha * residual
    new = residual - alpha * image
    new_ref[...] = new
    direction_ref[...] = new + (norm_new / one) * residual


def per_device(features, groups, targets, start):
    width, size = features.shape
    vectors = start.shape[0]
    planes = lax.axis_size(PLANE)
    lines = lax.axis_size(LINE)
    cores = lax.axis_size("core")
    scale = scale_of(width)
    amplitude = AMP_NUM / math.sqrt(size * planes * lines * cores)
    gain = -math.log2(RHO) / scale
    gains = constant_pieces(gain)
    shift = 0.5 * (math.log2(amplitude) / scale - gain)
    shape = jax.ShapeDtypeStruct

    def across(value):
        return lax.ppermute(value, "core", [(0, 1), (1, 0)])

    plane, line = pl.pallas_call(
        functools.partial(pack_body, shift=shift),
        out_shape=[shape((planes, HEAD, size), BF16), shape((lines, HEAD + vectors, size), BF16)],
        name="pack",
    )(features, groups.reshape(1, size), start)
    line = lax.all_to_all(line, LINE, 0, 0)
    plane = lax.all_to_all(plane, PLANE, 0, 0)
    far_line = across(line)
    tile, carried = build(line, plane, None, scale, gains, F32)
    far_tile, partial_value = build(far_line, plane, carried, scale, gains, BF16)
    received = lax.all_to_all(partial_value, PLANE, 0, 0)

    residual0, line_vector = pl.pallas_call(
        first_body,
        out_shape=[shape((vectors, size), F32), shape((lines, vectors, size), BF16)],
        name="first",
    )(received, targets, start)
    line_vector = lax.all_to_all(line_vector, LINE, 0, 0)
    far_vector = across(line_vector)
    carried = apply(line_vector, tile, None, F32)
    partial_value = apply(far_vector, far_tile, carried, BF16)
    received = lax.all_to_all(partial_value, PLANE, 0, 0)

    product, sums = pl.pallas_call(
        sums_body,
        out_shape=[shape((vectors, size), F32), shape((planes, 8, 128), F32)],
        name="sums",
    )(received, residual0)
    sums = lax.all_to_all(sums, PLANE, 0, 0)
    sums = pl.pallas_call(
        spread_body, out_shape=shape((lines, 8, 128), F32), name="spread"
    )(sums)
    sums = lax.all_to_all(sums, LINE, 0, 0)
    sums = pl.pallas_call(total_body, out_shape=shape((8, 128), F32), name="total")(sums)
    other = across(sums)
    return tuple(
        pl.pallas_call(
            last_body, out_shape=[shape((vectors, size), F32)] * 3, name="last"
        )(sums, other, start, residual0, product)
    )


def solution(mesh):
    fine = Mesh(mesh.devices.reshape(2, 4, 2, 8, 2), AXES)
    split = ("yh", "z", "core", "yl", "x")
    in_specs = (P(None, split), P(split), P(None, split), P(None, split))
    out_specs = (P(None, split),) * 3
    return jax.shard_map(
        per_device, mesh=fine, in_specs=in_specs, out_specs=out_specs, check_vma=False
    )
```

```python
import functools
import math

import jax
import jax.numpy as jnp
from jax import lax
from jax.experimental import pallas as pl
from jax.experimental.pallas import tpu as pltpu
from jax.sharding import Mesh, PartitionSpec as P

RHO = 0.2
AMP_NUM = 16.0

AXES = ("yl", "x", "yh", "z", "core")
ROW = ("yl", "x")
COL = ("yh", "z", "core")
LINE = ("z",)

BF16 = jnp.bfloat16
F32 = jnp.float32
VMEM = pl.BlockSpec(memory_space=pltpu.VMEM)

HEAD = 80
DEPTH = 128
WIDE = 512


def scale_of(width):
    return 2.0 * math.log2(math.e) / width


def pieces_of(value):
    first = value.astype(BF16).astype(F32)
    rest = value - first
    second = rest.astype(BF16).astype(F32)
    return first, second, rest - second


def constant_pieces(value):
    import numpy as np
    import ml_dtypes

    out = []
    rest = value
    for _ in range(3):
        piece = float(np.float32(rest).astype(ml_dtypes.bfloat16))
        out.append(piece)
        rest = rest - piece
    return out


def pack_body(features_ref, groups_ref, start_ref, plane_ref, line_ref, *, shift):
    features = features_ref[...]
    wide = features.astype(F32)
    half = shift - 0.5 * jnp.sum(wide * wide, axis=0, keepdims=True)
    first, second, third = pieces_of(half)
    group = groups_ref[...].astype(F32)
    count = features.shape[1]
    row = lax.broadcasted_iota(jnp.int32, (16, count), 0)
    tail = jnp.where(row == 0, first, 0.0)
    tail = jnp.where(row == 1, second, tail)
    tail = jnp.where(row == 2, third, tail)
    tail = jnp.where(row == 3, group, tail).astype(BF16)
    vector = start_ref[...].astype(BF16)
    for n in range(plane_ref.shape[0]):
        plane_ref[n, 0:64, :] = features
        plane_ref[n, 64:80, :] = tail
    for n in range(line_ref.shape[0]):
        line_ref[n, 0:64, :] = features
        line_ref[n, 64:80, :] = tail
        line_ref[n, 80:112, :] = vector


def tail_rows(packed, left, gains):
    count = packed.shape[1]
    head = packed.astype(F32)
    first, second, third, group = (head[n : n + 1, :] for n in range(4))
    row = lax.broadcasted_iota(jnp.int32, (64, count), 0)
    level = (row & 7).astype(F32)
    hot = jnp.where(level == group, 1.0, 0.0)
    if not left:
        hot = hot * jnp.where(row < 16, gains[0], jnp.where(row < 24, gains[1], gains[2]))
    out = jnp.where((row >= 8) & (row < 32), hot, 0.0)
    base = 0 if left else 3
    out = jnp.where((row >= 3 - base) & (row < 6 - base), 1.0, out)
    out = jnp.where(row == base, first, out)
    out = jnp.where(row == base + 1, second, out)
    out = jnp.where(row == base + 2, third, out)
    return out.astype(BF16)


def build_body(scale, gains, line_ref, plane_ref, carried_ref, tile_ref, out_ref, *scratch):
    left_ref, vector_ref, right_ref = scratch
    blocks, _, size = line_ref.shape
    per = WIDE // size
    for n in range(blocks):
        rows = line_ref[n, 0:64, :]
        tail = tail_rows(line_ref[n, 64:80, :], True, gains)
        left_ref[n * size : (n + 1) * size, :] = jnp.concatenate([rows, tail], axis=0).T
        vector_ref[:, n * size : (n + 1) * size] = line_ref[n, 80:112, :]

    def step(turn, state):
        columns = pl.ds(pl.multiple_of(turn * WIDE, WIDE), WIDE)
        for n in range(per):
            block = turn * per + n
            right_ref[0:64, n * size : (n + 1) * size] = plane_ref[block, 0:64, :]
            right_ref[64:128, n * size : (n + 1) * size] = tail_rows(
                plane_ref[block, 64:80, :], False, gains
            )
        right = right_ref[...]
        for n in range(blocks):
            power = jnp.dot(
                left_ref[n * size : (n + 1) * size, :], right, preferred_element_type=F32
            )
            tile_ref[n * size : (n + 1) * size, columns] = jnp.exp2(power * scale).astype(BF16)
        product = jnp.dot(
            vector_ref[...], tile_ref[:, columns], preferred_element_type=F32
        )
        for n in range(per):
            block = turn * per + n
            value = carried_ref[block] + product[:, n * size : (n + 1) * size]
            out_ref[block] = value.astype(out_ref.dtype)
        return state

    lax.fori_loop(0, plane_ref.shape[0] // per, step, 0)


def start_body(scale, gains, line_ref, plane_ref, tile_ref, out_ref, *scratch):
    out_ref[...] = jnp.zeros_like(out_ref)
    build_body(scale, gains, line_ref, plane_ref, out_ref, tile_ref, out_ref, *scratch)


def build(line, plane, carried, scale, gains, out_dtype):
    blocks, rows, size = line.shape
    columns = plane.shape[0]
    vectors = rows - HEAD
    points = blocks * size
    body = start_body if carried is None else build_body
    operands = [line, plane] + ([] if carried is None else [carried])
    return pl.pallas_call(
        functools.partial(body, scale, gains),
        in_specs=[VMEM] * len(operands),
        out_specs=[VMEM] * 2,
        out_shape=[
            pltpu.VMEM((points, columns * size), BF16),
            pltpu.VMEM((columns, vectors, size), out_dtype),
        ],
        scratch_shapes=[
            pltpu.VMEM((points, DEPTH), BF16),
            pltpu.VMEM((vectors, points), BF16),
            pltpu.VMEM((DEPTH, WIDE), BF16),
        ],
        compiler_params=pltpu.CompilerParams(vmem_limit_bytes=16 << 20),
        cost_estimate=pl.CostEstimate(
            flops=2 * points * columns * size * 512,
            bytes_accessed=2 * points * columns * size,
            transcendentals=points * columns * size,
        ),
        name="build",
    )(*operands)


def apply_body(vector_ref, tile_ref, *refs):
    out_ref, flat_ref = refs[-2:]
    blocks, _, size = vector_ref.shape
    for n in range(blocks):
        flat_ref[:, n * size : (n + 1) * size] = vector_ref[n]
    product = jnp.dot(flat_ref[...], tile_ref[...], preferred_element_type=F32)
    for n in range(out_ref.shape[0]):
        value = product[:, n * size : (n + 1) * size]
        if len(refs) == 3:
            value = value + refs[0][n]
        out_ref[n] = value.astype(out_ref.dtype)


def apply(vector, tile, carried, out_dtype):
    blocks, vectors, size = vector.shape
    points, total = tile.shape
    operands = [vector, tile] + ([] if carried is None else [carried])
    return pl.pallas_call(
        apply_body,
        in_specs=[VMEM] * len(operands),
        out_specs=VMEM,
        out_shape=pltpu.VMEM((total // size, vectors, size), out_dtype),
        scratch_shapes=[pltpu.VMEM((vectors, points), BF16)],
        compiler_params=pltpu.CompilerParams(vmem_limit_bytes=8 << 20),
        cost_estimate=pl.CostEstimate(
            flops=2 * points * total * 256,
            bytes_accessed=2 * points * total,
            transcendentals=0,
        ),
        name="apply",
    )(*operands)


def first_body(received_ref, targets_ref, start_ref, residual_ref, line_ref):
    product = jnp.sum(received_ref[...].astype(F32), axis=0)
    residual = targets_ref[...] - (start_ref[...] + product)
    residual_ref[...] = residual
    rounded = residual.astype(BF16)
    for n in range(line_ref.shape[0]):
        line_ref[n] = rounded


def sums_body(received_ref, residual_ref, product_ref, sums_ref):
    product = jnp.sum(received_ref[...].astype(F32), axis=0)
    product_ref[...] = product
    residual = residual_ref[...]
    vectors = residual.shape[0]
    one = jnp.sum(residual * residual, axis=1, keepdims=True)
    two = jnp.sum(residual * product, axis=1, keepdims=True)
    three = jnp.sum(product * product, axis=1, keepdims=True)
    lane = lax.broadcasted_iota(jnp.int32, (vectors, 128), 1)
    table = jnp.where(lane == 0, one, jnp.where(lane == 1, two, jnp.where(lane == 2, three, 0.0)))
    table = jnp.concatenate([table, jnp.zeros((128 - vectors, 128), F32)], axis=0).T[0:8, :]
    for n in range(sums_ref.shape[0]):
        sums_ref[n] = table


def spread_body(received_ref, sums_ref):
    table = jnp.sum(received_ref[...], axis=0)
    for n in range(sums_ref.shape[0]):
        sums_ref[n] = table


def last_body(
    received_ref, start_ref, residual_ref, product_ref, solution_ref, new_ref, direction_ref
):
    vectors = start_ref.shape[0]
    table = jnp.sum(received_ref[...], axis=0)
    table = jnp.concatenate([table, jnp.zeros((120, 128), F32)], axis=0).T[0:vectors, :]
    one, two, three = table[:, 0:1], table[:, 1:2], table[:, 2:3]
    alpha = one / (one + two)
    norm_new = alpha * alpha * jnp.maximum(three - two * two / one, 0.0)
    residual = residual_ref[...]
    image = residual + product_ref[...]
    solution_ref[...] = start_ref[...] + alpha * residual
    new = residual - alpha * image
    new_ref[...] = new
    direction_ref[...] = new + (norm_new / one) * residual


def small(body, name, outs, operands):
    return pl.pallas_call(
        body,
        in_specs=[VMEM] * len(operands),
        out_specs=[VMEM] * len(outs),
        out_shape=outs,
        compiler_params=pltpu.CompilerParams(vmem_limit_bytes=4 << 20),
        name=name,
    )(*operands)


def per_device(features, groups, targets, start):
    width, size = features.shape
    vectors = start.shape[0]
    rows = lax.axis_size(ROW)
    lines = lax.axis_size(LINE)
    columns = lax.axis_size(COL)
    scale = scale_of(width)
    amplitude = AMP_NUM / math.sqrt(size * rows * columns)
    gain = -math.log2(RHO) / scale
    gains = constant_pieces(gain)
    shift = 0.5 * (math.log2(amplitude) / scale - gain)

    def across(value, axis):
        return lax.ppermute(value, axis, [(0, 1), (1, 0)])

    plane, line = small(
        functools.partial(pack_body, shift=shift),
        "pack",
        [pltpu.VMEM((rows, HEAD, size), BF16), pltpu.VMEM((lines, HEAD + vectors, size), BF16)],
        [features, groups.reshape(1, size), start],
    )
    line = lax.all_to_all(line, LINE, 0, 0)
    far = across(line, "yh")
    near = across(line, "core")
    plane = lax.all_to_all(plane, ROW, 0, 0)
    tiles = [None] * 4
    tiles[0], carried = build(line, plane, None, scale, gains, F32)
    tiles[1], carried = build(near, plane, carried, scale, gains, F32)
    far, carried = lax.optimization_barrier((far, carried))
    last = across(far, "core")
    tiles[2], carried = build(far, plane, carried, scale, gains, F32)
    tiles[3], partial_value = build(last, plane, carried, scale, gains, BF16)
    received = lax.all_to_all(partial_value, ROW, 0, 0)

    residual0, vector = small(
        first_body,
        "first",
        [pltpu.VMEM((vectors, size), F32), pltpu.VMEM((lines, vectors, size), BF16)],
        [received, targets, start],
    )
    vector = lax.all_to_all(vector, LINE, 0, 0)
    far = across(vector, "yh")
    near = across(vector, "core")
    carried = apply(vector, tiles[0], None, F32)
    carried = apply(near, tiles[1], carried, F32)
    far, carried = lax.optimization_barrier((far, carried))
    last = across(far, "core")
    carried = apply(far, tiles[2], carried, F32)
    partial_value = apply(last, tiles[3], carried, BF16)
    received = lax.all_to_all(partial_value, ROW, 0, 0)

    product, sums = small(
        sums_body,
        "sums",
        [pltpu.VMEM((vectors, size), F32), pltpu.VMEM((rows, 8, 128), F32)],
        [received, residual0],
    )
    sums = lax.all_to_all(sums, ROW, 0, 0)
    (sums,) = small(spread_body, "spread", [pltpu.VMEM((columns, 8, 128), F32)], [sums])
    sums = lax.all_to_all(sums, COL, 0, 0)
    return tuple(
        small(
            last_body,
            "last",
            [jax.ShapeDtypeStruct((vectors, size), F32)] * 3,
            [sums, start, residual0, product],
        )
    )


def solution(mesh):
    fine = Mesh(mesh.devices.reshape(2, 4, 2, 8, 2), AXES)
    split = ("yh", "z", "core", "yl", "x")
    in_specs = (P(None, split), P(split), P(None, split), P(None, split))
    out_specs = (P(None, split),) * 3
    return jax.shard_map(
        per_device, mesh=fine, in_specs=in_specs, out_specs=out_specs, check_vma=False
    )
```

```python
import functools
import math

import jax
import jax.numpy as jnp
from jax import lax
from jax.experimental import pallas as pl
from jax.experimental.pallas import tpu as pltpu
from jax.sharding import Mesh, PartitionSpec as P

RHO = 0.2
AMP_NUM = 16.0

AXES = ("yl", "x", "yh", "z", "core")
ROW = ("x", "yl")
COL = ("yh", "z", "core")
LINE = ("z",)

BF16 = jnp.bfloat16
F32 = jnp.float32
VMEM = pl.BlockSpec(memory_space=pltpu.VMEM)
SMEM = pl.BlockSpec(memory_space=pltpu.SMEM)
HBM = pl.BlockSpec(memory_space=pltpu.HBM)

HEAD = 80
DEPTH = 128
WIDE = 1024


def scale_of(width):
    return 2.0 * math.log2(math.e) / width


def pieces_of(value):
    first = value.astype(BF16).astype(F32)
    rest = value - first
    second = rest.astype(BF16).astype(F32)
    return first, second, rest - second


def constant_pieces(value):
    import numpy as np
    import ml_dtypes

    out = []
    rest = value
    for _ in range(3):
        piece = float(np.float32(rest).astype(ml_dtypes.bfloat16))
        out.append(piece)
        rest = rest - piece
    return out


def pack_body(
    features_hbm, groups_hbm, start_hbm, own_ref, line_ref, features_ref, groups_ref, start_ref, sems,
    *, shift
):
    copies = [
        pltpu.make_async_copy(source, target, sems.at[n])
        for n, (source, target) in enumerate(
            ((features_hbm, features_ref), (groups_hbm, groups_ref), (start_hbm, start_ref))
        )
    ]
    for copy in copies:
        copy.start()
    for copy in copies:
        copy.wait()
    features = features_ref[...]
    wide = features.astype(F32)
    half = shift - 0.5 * jnp.sum(wide * wide, axis=0, keepdims=True)
    first, second, third = pieces_of(half)
    group = groups_ref[...].astype(F32)
    count = features.shape[1]
    row = lax.broadcasted_iota(jnp.int32, (16, count), 0)
    tail = jnp.where(row == 0, first, 0.0)
    tail = jnp.where(row == 1, second, tail)
    tail = jnp.where(row == 2, third, tail)
    tail = jnp.where(row == 3, group, tail).astype(BF16)
    vector = start_ref[...].astype(BF16)
    own_ref[0, 0:64, :] = features
    own_ref[0, 64:80, :] = tail
    for n in range(line_ref.shape[0]):
        line_ref[n, 0:64, :] = features
        line_ref[n, 64:80, :] = tail
        line_ref[n, 80:112, :] = vector


def tail_rows(packed, left, gains):
    count = packed.shape[1]
    head = packed.astype(F32)
    first, second, third, group = (head[n : n + 1, :] for n in range(4))
    row = lax.broadcasted_iota(jnp.int32, (64, count), 0)
    level = (row & 7).astype(F32)
    hot = jnp.where(level == group, 1.0, 0.0)
    if not left:
        hot = hot * jnp.where(row < 16, gains[0], jnp.where(row < 24, gains[1], gains[2]))
    out = jnp.where((row >= 8) & (row < 32), hot, 0.0)
    base = 0 if left else 3
    out = jnp.where((row >= 3 - base) & (row < 6 - base), 1.0, out)
    out = jnp.where(row == base, first, out)
    out = jnp.where(row == base + 1, second, out)
    out = jnp.where(row == base + 2, third, out)
    return out.astype(BF16)


def right_body(gains, *refs):
    right_ref = refs[-1]
    size = refs[0].shape[2]
    place = 0
    for ref in refs[:-1]:
        for n in range(ref.shape[0]):
            columns = slice(place * size, (place + 1) * size)
            right_ref[0:64, columns] = ref[n, 0:64, :]
            right_ref[64:128, columns] = tail_rows(ref[n, 64:80, :], False, gains)
            place += 1


def build_body(scale, me_ref, line_ref, right_ref, *refs, first, last):
    if not first:
        carried_ref, refs = refs[0], refs[1:]
    tile_ref, out_ref, left_ref, vector_ref = refs
    blocks, _, size = line_ref.shape
    per = WIDE // size
    for n in range(blocks):
        rows = line_ref[n, 0:64, :]
        tail = tail_rows(line_ref[n, 64:80, :], True, None)
        left_ref[n * size : (n + 1) * size, :] = jnp.concatenate([rows, tail], axis=0).T
        vector_ref[:, n * size : (n + 1) * size] = line_ref[n, 80:112, :]

    def step(turn, state):
        columns = pl.ds(pl.multiple_of(turn * WIDE, WIDE), WIDE)
        right = right_ref[:, columns]
        for n in range(blocks):
            power = jnp.dot(
                left_ref[n * size : (n + 1) * size, :], right, preferred_element_type=F32
            )
            tile_ref[n * size : (n + 1) * size, columns] = jnp.exp2(power * scale).astype(BF16)
        product = jnp.dot(
            vector_ref[...], tile_ref[:, columns], preferred_element_type=F32
        )
        for n in range(per):
            block = turn * per + n
            value = product[:, n * size : (n + 1) * size]
            if not first:
                value = value + carried_ref[block]
            if last:
                block = block ^ me_ref[0]
            out_ref[block] = value.astype(out_ref.dtype)
        return state

    lax.fori_loop(0, right_ref.shape[1] // WIDE, step, 0)


def build(line, right, carried, me, scale, last=False):
    blocks, rows, size = line.shape
    total = right.shape[1]
    vectors = rows - HEAD
    points = blocks * size
    first = carried is None
    operands, in_specs = [me, line, right], [SMEM, VMEM, VMEM]
    if not first:
        operands.append(carried)
        in_specs.append(VMEM)
    return pl.pallas_call(
        functools.partial(build_body, scale, first=first, last=last),
        in_specs=in_specs,
        out_specs=[VMEM] * 2,
        out_shape=[
            pltpu.VMEM((points, total), BF16),
            pltpu.VMEM((total // size, vectors, size), BF16 if last else F32),
        ],
        scratch_shapes=[pltpu.VMEM((points, DEPTH), BF16), pltpu.VMEM((vectors, points), BF16)],
        compiler_params=pltpu.CompilerParams(vmem_limit_bytes=6 << 20),
        cost_estimate=pl.CostEstimate(
            flops=2 * points * total * 512,
            bytes_accessed=2 * points * total,
            transcendentals=points * total,
        ),
        name="build",
    )(*operands)


def apply_body(vector_ref, tile_ref, *refs, first, last):
    if not first:
        carried_ref, refs = refs[0], refs[1:]
    if last:
        me_ref, refs = refs[0], refs[1:]
    out_ref, flat_ref = refs
    blocks, _, size = vector_ref.shape
    for n in range(blocks):
        flat_ref[:, n * size : (n + 1) * size] = vector_ref[n]
    product = jnp.dot(flat_ref[...], tile_ref[...], preferred_element_type=F32)
    for n in range(out_ref.shape[0]):
        value = product[:, n * size : (n + 1) * size]
        if not first:
            value = value + carried_ref[n]
        block = n ^ me_ref[0] if last else n
        out_ref[block] = value.astype(out_ref.dtype)


def apply(vector, tile, carried, me):
    blocks, vectors, size = vector.shape
    points, total = tile.shape
    first, last = carried is None, me is not None
    operands, in_specs = [vector, tile], [VMEM, VMEM]
    if not first:
        operands.append(carried)
        in_specs.append(VMEM)
    if last:
        operands.append(me)
        in_specs.append(SMEM)
    return pl.pallas_call(
        functools.partial(apply_body, first=first, last=last),
        in_specs=in_specs,
        out_specs=VMEM,
        out_shape=pltpu.VMEM((total // size, vectors, size), BF16 if last else F32),
        scratch_shapes=[pltpu.VMEM((vectors, points), BF16)],
        compiler_params=pltpu.CompilerParams(vmem_limit_bytes=4 << 20),
        cost_estimate=pl.CostEstimate(
            flops=2 * points * total * 256,
            bytes_accessed=2 * points * total,
            transcendentals=0,
        ),
        name="apply",
    )(*operands)


def first_body(received_ref, targets_ref, start_ref, residual_ref, line_ref):
    product = jnp.sum(received_ref[...].astype(F32), axis=0)
    residual = targets_ref[...] - (start_ref[...] + product)
    residual_ref[...] = residual
    rounded = residual.astype(BF16)
    for n in range(line_ref.shape[0]):
        line_ref[n] = rounded


def sums_body(received_ref, residual_ref, product_ref, sums_ref):
    product = jnp.sum(received_ref[...].astype(F32), axis=0)
    product_ref[...] = product
    residual = residual_ref[...]
    vectors = residual.shape[0]
    one = jnp.sum(residual * residual, axis=1, keepdims=True)
    two = jnp.sum(residual * product, axis=1, keepdims=True)
    three = jnp.sum(product * product, axis=1, keepdims=True)
    lane = lax.broadcasted_iota(jnp.int32, (vectors, 128), 1)
    table = jnp.where(lane == 0, one, jnp.where(lane == 1, two, jnp.where(lane == 2, three, 0.0)))
    table = jnp.concatenate([table, jnp.zeros((128 - vectors, 128), F32)], axis=0).T[0:8, :]
    for n in range(sums_ref.shape[0]):
        sums_ref[n] = table


def spread_body(received_ref, sums_ref):
    table = jnp.sum(received_ref[...], axis=0)
    for n in range(sums_ref.shape[0]):
        sums_ref[n] = table


def last_body(
    received_ref, start_ref, residual_ref, product_ref, solution_ref, new_ref, direction_ref
):
    vectors = start_ref.shape[0]
    table = jnp.sum(received_ref[...], axis=0)
    table = jnp.concatenate([table, jnp.zeros((120, 128), F32)], axis=0).T[0:vectors, :]
    one, two, three = table[:, 0:1], table[:, 1:2], table[:, 2:3]
    alpha = one / (one + two)
    norm_new = alpha * alpha * jnp.maximum(three - two * two / one, 0.0)
    residual = residual_ref[...]
    image = residual + product_ref[...]
    solution_ref[...] = start_ref[...] + alpha * residual
    new = residual - alpha * image
    new_ref[...] = new
    direction_ref[...] = new + (norm_new / one) * residual


def small(body, name, outs, operands):
    return pl.pallas_call(
        body,
        in_specs=[VMEM] * len(operands),
        out_specs=[VMEM] * len(outs),
        out_shape=outs,
        compiler_params=pltpu.CompilerParams(vmem_limit_bytes=4 << 20),
        name=name,
    )(*operands)


def per_device(features, groups, targets, start):
    width, size = features.shape
    vectors = start.shape[0]
    rows = lax.axis_size(ROW)
    lines = lax.axis_size(LINE)
    columns = lax.axis_size(COL)
    scale = scale_of(width)
    amplitude = AMP_NUM / math.sqrt(size * rows * columns)
    gain = -math.log2(RHO) / scale
    gains = constant_pieces(gain)
    shift = 0.5 * (math.log2(amplitude) / scale - gain)

    me = lax.axis_index(ROW).astype(jnp.int32).reshape(1)

    def across(value, axis, step=1):
        count = lax.axis_size(axis)
        return lax.ppermute(value, axis, [(n, n ^ step) for n in range(count)])

    own, line = pl.pallas_call(
        functools.partial(pack_body, shift=shift),
        in_specs=[HBM] * 3,
        out_specs=[VMEM] * 2,
        out_shape=[
            pltpu.VMEM((1, HEAD, size), BF16),
            pltpu.VMEM((lines, HEAD + vectors, size), BF16),
        ],
        scratch_shapes=[
            pltpu.VMEM((width, size), BF16),
            pltpu.VMEM((1, size), jnp.int32),
            pltpu.VMEM((vectors, size), F32),
            pltpu.SemaphoreType.DMA((3,)),
        ],
        compiler_params=pltpu.CompilerParams(vmem_limit_bytes=4 << 20),
        name="pack",
    )(features, groups.reshape(1, size), start)
    line = lax.all_to_all(line, LINE, 0, 0)
    pair = jnp.concatenate([own, across(own, "yl")], axis=0)
    parts = [pair] + [across(pair, "x", step) for step in (1, 2, 3)]
    (right,) = small(
        functools.partial(right_body, gains),
        "right",
        [pltpu.VMEM((DEPTH, rows * size), BF16)],
        parts,
    )
    line, right = lax.optimization_barrier((line, right))
    far = across(line, "yh")
    near = across(line, "core")
    tiles = [None] * 4
    tiles[0], carried = build(line, right, None, me, scale)
    tiles[1], carried = build(near, right, carried, me, scale)
    far, carried = lax.optimization_barrier((far, carried))
    last = across(far, "core")
    tiles[2], carried = build(far, right, carried, me, scale)
    tiles[3], partial_value = build(last, right, carried, me, scale, last=True)
    received = lax.all_to_all(partial_value, ROW, 0, 0)

    residual0, vector = small(
        first_body,
        "first",
        [pltpu.VMEM((vectors, size), F32), pltpu.VMEM((lines, vectors, size), BF16)],
        [received, targets, start],
    )
    vector = lax.all_to_all(vector, LINE, 0, 0)
    far = across(vector, "yh")
    near = across(vector, "core")
    carried = apply(vector, tiles[0], None, None)
    carried = apply(near, tiles[1], carried, None)
    far, carried = lax.optimization_barrier((far, carried))
    last = across(far, "core")
    carried = apply(far, tiles[2], carried, None)
    partial_value = apply(last, tiles[3], carried, me)
    received = lax.all_to_all(partial_value, ROW, 0, 0)

    product, sums = small(
        sums_body,
        "sums",
        [pltpu.VMEM((vectors, size), F32), pltpu.VMEM((rows, 8, 128), F32)],
        [received, residual0],
    )
    sums = lax.all_to_all(sums, ROW, 0, 0)
    (sums,) = small(spread_body, "spread", [pltpu.VMEM((columns, 8, 128), F32)], [sums])
    sums = lax.all_to_all(sums, COL, 0, 0)
    return tuple(
        small(
            last_body,
            "last",
            [jax.ShapeDtypeStruct((vectors, size), F32)] * 3,
            [sums, start, residual0, product],
        )
    )


def solution(mesh):
    fine = Mesh(mesh.devices.reshape(2, 4, 2, 8, 2), AXES)
    split = ("yh", "z", "core", "yl", "x")
    in_specs = (P(None, split), P(split), P(None, split), P(None, split))
    out_specs = (P(None, split),) * 3
    return jax.shard_map(
        per_device, mesh=fine, in_specs=in_specs, out_specs=out_specs, check_vma=False
    )
```

```python
import functools
import math

import jax
import jax.numpy as jnp
from jax import lax
from jax.experimental import pallas as pl
from jax.experimental.pallas import tpu as pltpu
from jax.sharding import Mesh, PartitionSpec as P

RHO = 0.2
AMP_NUM = 16.0

AXES = ("yl", "x", "yh", "z", "core")
ROW = ("x", "yl")
COL = ("yh", "z", "core")
LINE = ("z",)

BF16 = jnp.bfloat16
F32 = jnp.float32
VMEM = pl.BlockSpec(memory_space=pltpu.VMEM)
SMEM = pl.BlockSpec(memory_space=pltpu.SMEM)
HBM = pl.BlockSpec(memory_space=pltpu.HBM)

HEAD = 80
DEPTH = 128
WIDE = 1024


def scale_of(width):
    return 2.0 * math.log2(math.e) / width


def pieces_of(value):
    first = value.astype(BF16).astype(F32)
    rest = value - first
    second = rest.astype(BF16).astype(F32)
    return first, second, rest - second


def constant_pieces(value):
    import numpy as np
    import ml_dtypes

    out = []
    rest = value
    for _ in range(3):
        piece = float(np.float32(rest).astype(ml_dtypes.bfloat16))
        out.append(piece)
        rest = rest - piece
    return out


def pack_body(
    features_hbm, groups_hbm, start_hbm, own_ref, line_ref, features_ref, groups_ref, start_ref, sems,
    *, shift
):
    copies = [
        pltpu.make_async_copy(source, target, sems.at[n])
        for n, (source, target) in enumerate(
            ((features_hbm, features_ref), (groups_hbm, groups_ref), (start_hbm, start_ref))
        )
    ]
    for copy in copies:
        copy.start()
    for copy in copies:
        copy.wait()
    features = features_ref[...]
    wide = features.astype(F32)
    half = shift - 0.5 * jnp.sum(wide * wide, axis=0, keepdims=True)
    first, second, third = pieces_of(half)
    group = groups_ref[...].astype(F32)
    count = features.shape[1]
    row = lax.broadcasted_iota(jnp.int32, (16, count), 0)
    tail = jnp.where(row == 0, first, 0.0)
    tail = jnp.where(row == 1, second, tail)
    tail = jnp.where(row == 2, third, tail)
    tail = jnp.where(row == 3, group, tail).astype(BF16)
    vector = start_ref[...].astype(BF16)
    own_ref[0, 0:64, :] = features
    own_ref[0, 64:80, :] = tail
    for n in range(line_ref.shape[0]):
        line_ref[n, 0:64, :] = features
        line_ref[n, 64:80, :] = tail
        line_ref[n, 80:112, :] = vector


def tail_rows(packed, left, gains):
    count = packed.shape[1]
    head = packed.astype(F32)
    first, second, third, group = (head[n : n + 1, :] for n in range(4))
    row = lax.broadcasted_iota(jnp.int32, (64, count), 0)
    level = (row & 7).astype(F32)
    hot = jnp.where(level == group, 1.0, 0.0)
    if not left:
        hot = hot * jnp.where(row < 16, gains[0], jnp.where(row < 24, gains[1], gains[2]))
    out = jnp.where((row >= 8) & (row < 32), hot, 0.0)
    base = 0 if left else 3
    out = jnp.where((row >= 3 - base) & (row < 6 - base), 1.0, out)
    out = jnp.where(row == base, first, out)
    out = jnp.where(row == base + 1, second, out)
    out = jnp.where(row == base + 2, third, out)
    return out.astype(BF16)


def right_body(gains, *refs):
    right_ref = refs[-1]
    size = refs[0].shape[2]
    place = 0
    for ref in refs[:-1]:
        for n in range(ref.shape[0]):
            columns = slice(place * size, (place + 1) * size)
            right_ref[0:64, columns] = ref[n, 0:64, :]
            right_ref[64:128, columns] = tail_rows(ref[n, 64:80, :], False, gains)
            place += 1


def build_body(scale, me_ref, line_ref, right_ref, *refs, first, last):
    if not first:
        carried_ref, refs = refs[0], refs[1:]
    tile_ref, out_ref, left_ref, vector_ref = refs
    blocks, _, size = line_ref.shape
    per = WIDE // size
    for n in range(blocks):
        rows = line_ref[n, 0:64, :]
        tail = tail_rows(line_ref[n, 64:80, :], True, None)
        left_ref[n * size : (n + 1) * size, :] = jnp.concatenate([rows, tail], axis=0).T
        vector_ref[:, n * size : (n + 1) * size] = line_ref[n, 80:112, :]

    def step(turn, state):
        columns = pl.ds(pl.multiple_of(turn * WIDE, WIDE), WIDE)
        right = right_ref[:, columns]
        for n in range(blocks):
            power = jnp.dot(
                left_ref[n * size : (n + 1) * size, :], right, preferred_element_type=F32
            )
            tile_ref[n * size : (n + 1) * size, columns] = jnp.exp2(power * scale).astype(BF16)
        product = jnp.dot(
            vector_ref[...], tile_ref[:, columns], preferred_element_type=F32
        )
        for n in range(per):
            block = turn * per + n
            value = product[:, n * size : (n + 1) * size]
            if not first:
                value = value + carried_ref[block]
            if last:
                block = block ^ me_ref[0]
            out_ref[block] = value.astype(out_ref.dtype)
        return state

    lax.fori_loop(0, right_ref.shape[1] // WIDE, step, 0)


def build(line, right, carried, me, scale, last=False):
    blocks, rows, size = line.shape
    total = right.shape[1]
    vectors = rows - HEAD
    points = blocks * size
    first = carried is None
    operands, in_specs = [me, line, right], [SMEM, VMEM, VMEM]
    if not first:
        operands.append(carried)
        in_specs.append(VMEM)
    return pl.pallas_call(
        functools.partial(build_body, scale, first=first, last=last),
        in_specs=in_specs,
        out_specs=[VMEM] * 2,
        out_shape=[
            pltpu.VMEM((points, total), BF16),
            pltpu.VMEM((total // size, vectors, size), BF16 if last else F32),
        ],
        scratch_shapes=[pltpu.VMEM((points, DEPTH), BF16), pltpu.VMEM((vectors, points), BF16)],
        compiler_params=pltpu.CompilerParams(vmem_limit_bytes=6 << 20),
        cost_estimate=pl.CostEstimate(
            flops=2 * points * total * 512,
            bytes_accessed=2 * points * total,
            transcendentals=points * total,
        ),
        name="build",
    )(*operands)


def apply_body(vector_ref, tile_ref, *refs, first, last):
    if not first:
        carried_ref, refs = refs[0], refs[1:]
    if last:
        me_ref, refs = refs[0], refs[1:]
    out_ref, flat_ref = refs
    blocks, _, size = vector_ref.shape
    for n in range(blocks):
        flat_ref[:, n * size : (n + 1) * size] = vector_ref[n]
    product = jnp.dot(flat_ref[...], tile_ref[...], preferred_element_type=F32)
    for n in range(out_ref.shape[0]):
        value = product[:, n * size : (n + 1) * size]
        if not first:
            value = value + carried_ref[n]
        block = n ^ me_ref[0] if last else n
        out_ref[block] = value.astype(out_ref.dtype)


def apply(vector, tile, carried, me):
    blocks, vectors, size = vector.shape
    points, total = tile.shape
    first, last = carried is None, me is not None
    operands, in_specs = [vector, tile], [VMEM, VMEM]
    if not first:
        operands.append(carried)
        in_specs.append(VMEM)
    if last:
        operands.append(me)
        in_specs.append(SMEM)
    return pl.pallas_call(
        functools.partial(apply_body, first=first, last=last),
        in_specs=in_specs,
        out_specs=VMEM,
        out_shape=pltpu.VMEM((total // size, vectors, size), BF16 if last else F32),
        scratch_shapes=[pltpu.VMEM((vectors, points), BF16)],
        compiler_params=pltpu.CompilerParams(vmem_limit_bytes=4 << 20),
        cost_estimate=pl.CostEstimate(
            flops=2 * points * total * 256,
            bytes_accessed=2 * points * total,
            transcendentals=0,
        ),
        name="apply",
    )(*operands)


def first_body(received_ref, targets_ref, start_ref, residual_ref, line_ref):
    product = jnp.sum(received_ref[...].astype(F32), axis=0)
    residual = targets_ref[...] - (start_ref[...] + product)
    residual_ref[...] = residual
    rounded = residual.astype(BF16)
    for n in range(line_ref.shape[0]):
        line_ref[n] = rounded


def sums_body(received_ref, residual_ref, product_ref, sums_ref):
    product = jnp.sum(received_ref[...].astype(F32), axis=0)
    product_ref[...] = product
    residual = residual_ref[...]
    vectors = residual.shape[0]
    one = jnp.sum(residual * residual, axis=1, keepdims=True)
    two = jnp.sum(residual * product, axis=1, keepdims=True)
    three = jnp.sum(product * product, axis=1, keepdims=True)
    lane = lax.broadcasted_iota(jnp.int32, (vectors, 128), 1)
    table = jnp.where(lane == 0, one, jnp.where(lane == 1, two, jnp.where(lane == 2, three, 0.0)))
    table = jnp.concatenate([table, jnp.zeros((128 - vectors, 128), F32)], axis=0).T[0:8, :]
    for n in range(sums_ref.shape[0]):
        sums_ref[n] = table


def spread_body(received_ref, sums_ref):
    table = jnp.sum(received_ref[...], axis=0)
    for n in range(sums_ref.shape[0]):
        sums_ref[n] = table


def last_body(
    received_ref, start_ref, residual_ref, product_ref, solution_ref, new_ref, direction_ref
):
    vectors = start_ref.shape[0]
    table = jnp.sum(received_ref[...], axis=0)
    table = jnp.concatenate([table, jnp.zeros((120, 128), F32)], axis=0).T[0:vectors, :]
    one, two, three = table[:, 0:1], table[:, 1:2], table[:, 2:3]
    alpha = one / (one + two)
    norm_new = alpha * alpha * jnp.maximum(three - two * two / one, 0.0)
    residual = residual_ref[...]
    image = residual + product_ref[...]
    solution_ref[...] = start_ref[...] + alpha * residual
    new = residual - alpha * image
    new_ref[...] = new
    direction_ref[...] = new + (norm_new / one) * residual


def small(body, name, outs, operands):
    return pl.pallas_call(
        body,
        in_specs=[VMEM] * len(operands),
        out_specs=[VMEM] * len(outs),
        out_shape=outs,
        compiler_params=pltpu.CompilerParams(vmem_limit_bytes=4 << 20),
        name=name,
    )(*operands)


def per_device(features, groups, targets, start):
    width, size = features.shape
    vectors = start.shape[0]
    rows = lax.axis_size(ROW)
    lines = lax.axis_size(LINE)
    columns = lax.axis_size(COL)
    scale = scale_of(width)
    amplitude = AMP_NUM / math.sqrt(size * rows * columns)
    gain = -math.log2(RHO) / scale
    gains = constant_pieces(gain)
    shift = 0.5 * (math.log2(amplitude) / scale - gain)

    me = lax.axis_index(ROW).astype(jnp.int32).reshape(1)

    def across(value, axis, step=1):
        count = lax.axis_size(axis)
        return lax.ppermute(value, axis, [(n, n ^ step) for n in range(count)])

    own, line = pl.pallas_call(
        functools.partial(pack_body, shift=shift),
        in_specs=[HBM] * 3,
        out_shape=[
            jax.ShapeDtypeStruct((1, HEAD, size), BF16),
            jax.ShapeDtypeStruct((lines, HEAD + vectors, size), BF16),
        ],
        scratch_shapes=[
            pltpu.VMEM((width, size), BF16),
            pltpu.VMEM((1, size), jnp.int32),
            pltpu.VMEM((vectors, size), F32),
            pltpu.SemaphoreType.DMA((3,)),
        ],
        name="pack",
    )(features, groups.reshape(1, size), start)
    line = lax.all_to_all(line, LINE, 0, 0)
    pair = jnp.concatenate([own, across(own, "yl")], axis=0)
    parts = [pair] + [across(pair, "x", step) for step in (1, 2, 3)]
    (right,) = small(
        functools.partial(right_body, gains),
        "right",
        [pltpu.VMEM((DEPTH, rows * size), BF16)],
        parts,
    )
    line, right = lax.optimization_barrier((line, right))
    far = across(line, "yh")
    near = across(line, "core")
    tiles = [None] * 4
    tiles[0], carried = build(line, right, None, me, scale)
    tiles[1], carried = build(near, right, carried, me, scale)
    far, carried = lax.optimization_barrier((far, carried))
    last = across(far, "core")
    tiles[2], carried = build(far, right, carried, me, scale)
    tiles[3], partial_value = build(last, right, carried, me, scale, last=True)
    received = lax.all_to_all(partial_value, ROW, 0, 0)

    residual0, vector = small(
        first_body,
        "first",
        [pltpu.VMEM((vectors, size), F32), pltpu.VMEM((lines, vectors, size), BF16)],
        [received, targets, start],
    )
    vector = lax.all_to_all(vector, LINE, 0, 0)
    far = across(vector, "yh")
    near = across(vector, "core")
    carried = apply(vector, tiles[0], None, None)
    carried = apply(near, tiles[1], carried, None)
    far, carried = lax.optimization_barrier((far, carried))
    last = across(far, "core")
    carried = apply(far, tiles[2], carried, None)
    partial_value = apply(last, tiles[3], carried, me)
    received = lax.all_to_all(partial_value, ROW, 0, 0)

    product, sums = small(
        sums_body,
        "sums",
        [pltpu.VMEM((vectors, size), F32), pltpu.VMEM((rows, 8, 128), F32)],
        [received, residual0],
    )
    sums = lax.all_to_all(sums, ('x', 'core'), 0, 0)
    (sums,) = small(spread_body, "spread", [pltpu.VMEM((columns, 8, 128), F32)], [sums])
    sums = lax.all_to_all(sums, ('yl', 'yh', 'z'), 0, 0)
    return tuple(
        small(
            last_body,
            "last",
            [jax.ShapeDtypeStruct((vectors, size), F32)] * 3,
            [sums, start, residual0, product],
        )
    )


def solution(mesh):
    fine = Mesh(mesh.devices.reshape(2, 4, 2, 8, 2), AXES)
    split = ("yh", "z", "core", "yl", "x")
    in_specs = (P(None, split), P(split), P(None, split), P(None, split))
    out_specs = (P(None, split),) * 3
    return jax.shard_map(
        per_device, mesh=fine, in_specs=in_specs, out_specs=out_specs, check_vma=False
    )
```

```python
import functools
import math

import jax
import jax.numpy as jnp
from jax import lax
from jax.experimental import pallas as pl
from jax.experimental.pallas import tpu as pltpu
from jax.sharding import Mesh, PartitionSpec as P

RHO = 0.2
AMP_NUM = 16.0

AXES = ("yl", "x", "yh", "z", "core")
PLANE = ("x", "yl", "yh")
LINE = ("z",)

BF16 = jnp.bfloat16
F32 = jnp.float32
VMEM = pl.BlockSpec(memory_space=pltpu.VMEM)
SMEM = pl.BlockSpec(memory_space=pltpu.SMEM)
HBM = pl.BlockSpec(memory_space=pltpu.HBM)

HEAD = 80
DEPTH = 128


def scale_of(width):
    return 2.0 * math.log2(math.e) / width


def pieces_of(value):
    first = value.astype(BF16).astype(F32)
    rest = value - first
    second = rest.astype(BF16).astype(F32)
    return first, second, rest - second


def constant_pieces(value):
    import numpy as np
    import ml_dtypes

    out = []
    rest = value
    for _ in range(3):
        piece = float(np.float32(rest).astype(ml_dtypes.bfloat16))
        out.append(piece)
        rest = rest - piece
    return out


def pack_body(
    features_hbm, groups_hbm, start_hbm, own_ref, line_ref, features_ref, groups_ref, start_ref, sems,
    *, shift
):
    copies = [
        pltpu.make_async_copy(source, target, sems.at[n])
        for n, (source, target) in enumerate(
            ((features_hbm, features_ref), (groups_hbm, groups_ref), (start_hbm, start_ref))
        )
    ]
    for copy in copies:
        copy.start()
    for copy in copies:
        copy.wait()
    features = features_ref[...]
    wide = features.astype(F32)
    half = shift - 0.5 * jnp.sum(wide * wide, axis=0, keepdims=True)
    first, second, third = pieces_of(half)
    group = groups_ref[...].astype(F32)
    count = features.shape[1]
    row = lax.broadcasted_iota(jnp.int32, (16, count), 0)
    tail = jnp.where(row == 0, first, 0.0)
    tail = jnp.where(row == 1, second, tail)
    tail = jnp.where(row == 2, third, tail)
    tail = jnp.where(row == 3, group, tail).astype(BF16)
    vector = start_ref[...].astype(BF16)
    own_ref[0, 0:64, :] = features
    own_ref[0, 64:80, :] = tail
    for n in range(line_ref.shape[0]):
        line_ref[n, 0:64, :] = features
        line_ref[n, 64:80, :] = tail
        line_ref[n, 80:112, :] = vector


def tail_rows(packed, left, gains):
    count = packed.shape[1]
    head = packed.astype(F32)
    first, second, third, group = (head[n : n + 1, :] for n in range(4))
    row = lax.broadcasted_iota(jnp.int32, (64, count), 0)
    level = (row & 7).astype(F32)
    hot = jnp.where(level == group, 1.0, 0.0)
    if not left:
        hot = hot * jnp.where(row < 16, gains[0], jnp.where(row < 24, gains[1], gains[2]))
    out = jnp.where((row >= 8) & (row < 32), hot, 0.0)
    base = 0 if left else 3
    out = jnp.where((row >= 3 - base) & (row < 6 - base), 1.0, out)
    out = jnp.where(row == base, first, out)
    out = jnp.where(row == base + 1, second, out)
    out = jnp.where(row == base + 2, third, out)
    return out.astype(BF16)


def right_body(gains, block_ref, right_ref):
    size = block_ref.shape[2]
    for n in range(block_ref.shape[0]):
        columns = slice(n * size, (n + 1) * size)
        right_ref[0:64, columns] = block_ref[n, 0:64, :]
        right_ref[64:128, columns] = tail_rows(block_ref[n, 64:80, :], False, gains)


def left_body(me_ref, line_ref, left_ref, vector_ref):
    blocks, _, size = line_ref.shape
    for n in range(blocks):
        rows = line_ref[n, 0:64, :]
        tail = tail_rows(line_ref[n, 64:80, :], True, None)
        left_ref[n * size : (n + 1) * size, :] = jnp.concatenate([rows, tail], axis=0).T
        vector_ref[:, n * size : (n + 1) * size] = line_ref[n, 80:112, :]


def build_body(scale, *refs, groups, last):
    if last:
        me_ref, refs = refs[0], refs[1:]
    left_ref, vector_ref, right_refs, refs = refs[0], refs[1], refs[2 : 2 + groups], refs[2 + groups :]
    carried_refs, tile_refs, out_ref = refs[: -groups - 1], refs[-groups - 1 : -1], refs[-1]
    points = left_ref.shape[0]
    size = out_ref.shape[2]
    place = 0
    for group in range(groups):
        right = right_refs[group][...]
        tile_ref = tile_refs[group]
        for n in range(0, points, 256):
            power = jnp.dot(left_ref[n : n + 256, :], right, preferred_element_type=F32)
            tile_ref[n : n + 256, :] = jnp.exp2(power * scale).astype(BF16)
        product = jnp.dot(vector_ref[...], tile_ref[...], preferred_element_type=F32)
        for n in range(product.shape[1] // size):
            value = product[:, n * size : (n + 1) * size]
            if last:
                value = (value + carried_refs[group][n]).astype(out_ref.dtype)
                out_ref[place ^ me_ref[0]] = value
            else:
                out_ref[place] = value
            place += 1


def build(left, vector, rights, carried, size, scale, me):
    points, wide = left.shape[0], rights[0].shape[1]
    vectors = vector.shape[0]
    last = carried is not None
    operands = [left, vector] + rights
    in_specs = [VMEM] * len(operands)
    if last:
        operands = [me] + operands + carried
        in_specs = [SMEM] + in_specs + [VMEM] * len(carried)
    total = len(rights) * wide
    outs = pl.pallas_call(
        functools.partial(build_body, scale, groups=len(rights), last=last),
        in_specs=in_specs,
        out_specs=[VMEM] * (len(rights) + 1),
        out_shape=[pltpu.VMEM((points, wide), BF16)] * len(rights)
        + [pltpu.VMEM((total // size, vectors, size), BF16 if last else F32)],
        compiler_params=pltpu.CompilerParams(vmem_limit_bytes=8 << 20),
        cost_estimate=pl.CostEstimate(
            flops=2 * points * total * 512,
            bytes_accessed=2 * points * total,
            transcendentals=points * total,
        ),
        name="build",
    )(*operands)
    return list(outs[:-1]), outs[-1]


def apply_body(*refs, tiles, last):
    if last:
        me_ref, refs = refs[0], refs[1:]
    vector_ref, tile_refs, refs = refs[0], refs[1 : 1 + tiles], refs[1 + tiles :]
    out_ref, flat_ref = refs[-2:]
    blocks, _, size = vector_ref.shape
    for n in range(blocks):
        flat_ref[:, n * size : (n + 1) * size] = vector_ref[n]
    place = 0
    for tile_ref in tile_refs:
        product = jnp.dot(flat_ref[...], tile_ref[...], preferred_element_type=F32)
        for n in range(product.shape[1] // size):
            value = product[:, n * size : (n + 1) * size]
            if last:
                out_ref[place ^ me_ref[0]] = (value + refs[0][place]).astype(out_ref.dtype)
            else:
                out_ref[place] = value
            place += 1


def apply(vector, tiles, carried, me):
    blocks, vectors, size = vector.shape
    points, wide = tiles[0].shape
    last = carried is not None
    operands = [vector] + tiles
    in_specs = [VMEM] * len(operands)
    if last:
        operands = [me] + operands + [carried]
        in_specs = [SMEM] + in_specs + [VMEM]
    total = len(tiles) * wide
    return pl.pallas_call(
        functools.partial(apply_body, tiles=len(tiles), last=last),
        in_specs=in_specs,
        out_specs=VMEM,
        out_shape=pltpu.VMEM((total // size, vectors, size), BF16 if last else F32),
        scratch_shapes=[pltpu.VMEM((vectors, points), BF16)],
        compiler_params=pltpu.CompilerParams(vmem_limit_bytes=4 << 20),
        cost_estimate=pl.CostEstimate(
            flops=2 * points * total * 256,
            bytes_accessed=2 * points * total,
            transcendentals=0,
        ),
        name="apply",
    )(*operands)


def first_body(received_ref, targets_ref, start_ref, residual_ref, line_ref):
    product = jnp.sum(received_ref[...].astype(F32), axis=0)
    residual = targets_ref[...] - (start_ref[...] + product)
    residual_ref[...] = residual
    rounded = residual.astype(BF16)
    for n in range(line_ref.shape[0]):
        line_ref[n] = rounded


def sums_body(received_ref, residual_ref, product_ref, sums_ref):
    product = jnp.sum(received_ref[...].astype(F32), axis=0)
    product_ref[...] = product
    residual = residual_ref[...]
    vectors = residual.shape[0]
    one = jnp.sum(residual * residual, axis=1, keepdims=True)
    two = jnp.sum(residual * product, axis=1, keepdims=True)
    three = jnp.sum(product * product, axis=1, keepdims=True)
    lane = lax.broadcasted_iota(jnp.int32, (vectors, 128), 1)
    table = jnp.where(lane == 0, one, jnp.where(lane == 1, two, jnp.where(lane == 2, three, 0.0)))
    table = jnp.concatenate([table, jnp.zeros((128 - vectors, 128), F32)], axis=0).T[0:8, :]
    for n in range(sums_ref.shape[0]):
        sums_ref[n] = table


def spread_body(received_ref, sums_ref):
    table = jnp.sum(received_ref[...], axis=0)
    for n in range(sums_ref.shape[0]):
        sums_ref[n] = table


def last_body(
    received_ref, start_ref, residual_ref, product_ref, solution_ref, new_ref, direction_ref
):
    vectors = start_ref.shape[0]
    table = jnp.sum(received_ref[...], axis=0)
    table = jnp.concatenate([table, jnp.zeros((120, 128), F32)], axis=0).T[0:vectors, :]
    one, two, three = table[:, 0:1], table[:, 1:2], table[:, 2:3]
    alpha = one / (one + two)
    norm_new = alpha * alpha * jnp.maximum(three - two * two / one, 0.0)
    residual = residual_ref[...]
    image = residual + product_ref[...]
    solution_ref[...] = start_ref[...] + alpha * residual
    new = residual - alpha * image
    new_ref[...] = new
    direction_ref[...] = new + (norm_new / one) * residual


def small(body, name, outs, operands):
    return pl.pallas_call(
        body,
        in_specs=[SMEM if operand.size == 1 else VMEM for operand in operands],
        out_specs=[VMEM] * len(outs),
        out_shape=outs,
        compiler_params=pltpu.CompilerParams(vmem_limit_bytes=4 << 20),
        name=name,
    )(*operands)


def per_device(features, groups, targets, start):
    width, size = features.shape
    vectors = start.shape[0]
    planes = lax.axis_size(PLANE)
    lines = lax.axis_size(LINE)
    scale = scale_of(width)
    amplitude = AMP_NUM / math.sqrt(size * planes * lines * lax.axis_size("core"))
    gain = -math.log2(RHO) / scale
    gains = constant_pieces(gain)
    shift = 0.5 * (math.log2(amplitude) / scale - gain)

    me = lax.axis_index(PLANE).astype(jnp.int32).reshape(1)

    def across(value, axis, step=1):
        count = lax.axis_size(axis)
        return lax.ppermute(value, axis, [(n, n ^ step) for n in range(count)])

    own, line = pl.pallas_call(
        functools.partial(pack_body, shift=shift),
        in_specs=[HBM] * 3,
        out_shape=[
            jax.ShapeDtypeStruct((1, HEAD, size), BF16),
            jax.ShapeDtypeStruct((lines, HEAD + vectors, size), BF16),
        ],
        scratch_shapes=[
            pltpu.VMEM((width, size), BF16),
            pltpu.VMEM((1, size), jnp.int32),
            pltpu.VMEM((vectors, size), F32),
            pltpu.SemaphoreType.DMA((3,)),
        ],
        name="pack",
    )(features, groups.reshape(1, size), start)
    line = lax.all_to_all(line, LINE, 0, 0)
    side = [own] + [across(own, ("yl", "yh"), step) for step in (1, 2, 3)]
    side = jnp.concatenate(side, axis=0)
    parts = [side] + [across(side, "x", step) for step in (1, 2, 3)]

    def right_of(part):
        (out,) = small(
            functools.partial(right_body, gains),
            "right",
            [pltpu.VMEM((DEPTH, part.shape[0] * size), BF16)],
            [part],
        )
        return out

    def left_of(value):
        points = value.shape[0] * size
        return small(
            left_body,
            "left",
            [pltpu.VMEM((points, DEPTH), BF16), pltpu.VMEM((vectors, points), BF16)],
            [me, value],
        )

    rights = [right_of(parts[0])]
    line, rights[0] = lax.optimization_barrier((line, rights[0]))
    near = across(line, "core")
    left, vector = left_of(line)
    tiles, carried = [None] * 4, [None] * 4
    for n in range(4):
        if n > 0:
            left, part = lax.optimization_barrier((left, parts[n]))
            rights.append(right_of(part))
        (tiles[n],), carried[n] = build(left, vector, [rights[n]], None, size, scale, me)
        left, carried[n] = lax.optimization_barrier((left, carried[n]))
    near, carried[3] = lax.optimization_barrier((near, carried[3]))
    left, vector = left_of(near)
    near_tiles, partial_value = build(left, vector, rights, carried, size, scale, me)
    received = lax.all_to_all(partial_value, PLANE, 0, 0)

    residual0, vector = small(
        first_body,
        "first",
        [pltpu.VMEM((vectors, size), F32), pltpu.VMEM((lines, vectors, size), BF16)],
        [received, targets, start],
    )
    vector = lax.all_to_all(vector, LINE, 0, 0)
    near = across(vector, "core")
    total = apply(vector, tiles, None, me)
    partial_value = apply(near, near_tiles, total, me)
    received = lax.all_to_all(partial_value, PLANE, 0, 0)

    product, sums = small(
        sums_body,
        "sums",
        [pltpu.VMEM((vectors, size), F32), pltpu.VMEM((8, 8, 128), F32)],
        [received, residual0],
    )
    sums = lax.all_to_all(sums, ('x', 'core'), 0, 0)
    (sums,) = small(spread_body, "spread", [pltpu.VMEM((32, 8, 128), F32)], [sums])
    sums = lax.all_to_all(sums, ('yl', 'yh', 'z'), 0, 0)
    return tuple(
        small(
            last_body,
            "last",
            [jax.ShapeDtypeStruct((vectors, size), F32)] * 3,
            [sums, start, residual0, product],
        )
    )


def solution(mesh):
    fine = Mesh(mesh.devices.reshape(2, 4, 2, 8, 2), AXES)
    split = ("yh", "z", "core", "yl", "x")
    in_specs = (P(None, split), P(split), P(None, split), P(None, split))
    out_specs = (P(None, split),) * 3
    return jax.shard_map(
        per_device, mesh=fine, in_specs=in_specs, out_specs=out_specs, check_vma=False
    )
```

```python
import functools
import math

import jax
import jax.numpy as jnp
from jax import lax
from jax.experimental import pallas as pl
from jax.experimental.pallas import tpu as pltpu
from jax.sharding import Mesh, PartitionSpec as P

RHO = 0.2
AMP_NUM = 16.0

AXES = ("yl", "x", "yh", "z", "core")
PLANE = ("x", "yl", "yh")
LINE = ("z",)

BF16 = jnp.bfloat16
F32 = jnp.float32
VMEM = pl.BlockSpec(memory_space=pltpu.VMEM)
SMEM = pl.BlockSpec(memory_space=pltpu.SMEM)
HBM = pl.BlockSpec(memory_space=pltpu.HBM)

HEAD = 80
DEPTH = 128


def scale_of(width):
    return 2.0 * math.log2(math.e) / width


def pieces_of(value):
    first = value.astype(BF16).astype(F32)
    rest = value - first
    second = rest.astype(BF16).astype(F32)
    return first, second, rest - second


def constant_pieces(value):
    import numpy as np
    import ml_dtypes

    out = []
    rest = value
    for _ in range(3):
        piece = float(np.float32(rest).astype(ml_dtypes.bfloat16))
        out.append(piece)
        rest = rest - piece
    return out


def pack_body(
    features_hbm, groups_hbm, start_hbm, own_ref, line_ref, features_ref, groups_ref, start_ref, sems,
    *, shift
):
    copies = [
        pltpu.make_async_copy(source, target, sems.at[n])
        for n, (source, target) in enumerate(
            ((features_hbm, features_ref), (groups_hbm, groups_ref), (start_hbm, start_ref))
        )
    ]
    for copy in copies:
        copy.start()
    for copy in copies:
        copy.wait()
    features = features_ref[...]
    wide = features.astype(F32)
    half = shift - 0.5 * jnp.sum(wide * wide, axis=0, keepdims=True)
    first, second, third = pieces_of(half)
    group = groups_ref[...].astype(F32)
    count = features.shape[1]
    row = lax.broadcasted_iota(jnp.int32, (16, count), 0)
    tail = jnp.where(row == 0, first, 0.0)
    tail = jnp.where(row == 1, second, tail)
    tail = jnp.where(row == 2, third, tail)
    tail = jnp.where(row == 3, group, tail).astype(BF16)
    vector = start_ref[...].astype(BF16)
    own_ref[0, 0:64, :] = features
    own_ref[0, 64:80, :] = tail
    for n in range(line_ref.shape[0]):
        line_ref[n, 0:64, :] = features
        line_ref[n, 64:80, :] = tail
        line_ref[n, 80:112, :] = vector


def tail_rows(packed, left, gains):
    count = packed.shape[1]
    head = packed.astype(F32)
    first, second, third, group = (head[n : n + 1, :] for n in range(4))
    row = lax.broadcasted_iota(jnp.int32, (64, count), 0)
    level = (row & 7).astype(F32)
    hot = jnp.where(level == group, 1.0, 0.0)
    if not left:
        hot = hot * jnp.where(row < 16, gains[0], jnp.where(row < 24, gains[1], gains[2]))
    out = jnp.where((row >= 8) & (row < 32), hot, 0.0)
    base = 0 if left else 3
    out = jnp.where((row >= 3 - base) & (row < 6 - base), 1.0, out)
    out = jnp.where(row == base, first, out)
    out = jnp.where(row == base + 1, second, out)
    out = jnp.where(row == base + 2, third, out)
    return out.astype(BF16)


def right_body(gains, block_ref, right_ref):
    size = block_ref.shape[2]
    for n in range(block_ref.shape[0]):
        columns = slice(n * size, (n + 1) * size)
        right_ref[0:64, columns] = block_ref[n, 0:64, :]
        right_ref[64:128, columns] = tail_rows(block_ref[n, 64:80, :], False, gains)


def left_body(me_ref, line_ref, left_ref, vector_ref):
    blocks, _, size = line_ref.shape
    for n in range(blocks):
        rows = line_ref[n, 0:64, :]
        tail = tail_rows(line_ref[n, 64:80, :], True, None)
        left_ref[n * size : (n + 1) * size, :] = jnp.concatenate([rows, tail], axis=0).T
        vector_ref[:, n * size : (n + 1) * size] = line_ref[n, 80:112, :]


def build_body(scale, *refs, groups, last):
    if last:
        me_ref, refs = refs[0], refs[1:]
    left_ref, vector_ref, right_refs, refs = refs[0], refs[1], refs[2 : 2 + groups], refs[2 + groups :]
    carried_refs, tile_refs, out_ref = refs[: -groups - 1], refs[-groups - 1 : -1], refs[-1]
    points = left_ref.shape[0]
    size = out_ref.shape[2]
    place = 0

    def put(value):
        if last:
            out_ref[place ^ me_ref[0]] = value.astype(out_ref.dtype)
        else:
            out_ref[place] = value

    if last:
        for n in range(carried_refs[0].shape[0]):
            put(carried_refs[0][n])
            place += 1
        carried_refs = carried_refs[1:]
    for group in range(groups):
        right = right_refs[group][...]
        tile_ref = tile_refs[group]
        for n in range(0, points, 256):
            power = jnp.dot(left_ref[n : n + 256, :], right, preferred_element_type=F32)
            tile_ref[n : n + 256, :] = jnp.exp2(power * scale).astype(BF16)
        product = jnp.dot(vector_ref[...], tile_ref[...], preferred_element_type=F32)
        for n in range(product.shape[1] // size):
            value = product[:, n * size : (n + 1) * size]
            if carried_refs:
                value = value + carried_refs[group][n]
            put(value)
            place += 1


def build(left, vector, rights, carried, size, scale, me, last=False):
    points, wide = left.shape[0], rights[0].shape[1]
    vectors = vector.shape[0]
    operands = [left, vector] + rights + carried
    in_specs = [VMEM] * len(operands)
    if last:
        operands = [me] + operands
        in_specs = [SMEM] + in_specs
    total = len(rights) * wide
    blocks = total // size + (carried[0].shape[0] if last else 0)
    outs = pl.pallas_call(
        functools.partial(build_body, scale, groups=len(rights), last=last),
        in_specs=in_specs,
        out_specs=[VMEM] * (len(rights) + 1),
        out_shape=[pltpu.VMEM((points, wide), BF16)] * len(rights)
        + [pltpu.VMEM((blocks, vectors, size), BF16 if last else F32)],
        compiler_params=pltpu.CompilerParams(vmem_limit_bytes=8 << 20),
        cost_estimate=pl.CostEstimate(
            flops=2 * points * total * 512,
            bytes_accessed=2 * points * total,
            transcendentals=points * total,
        ),
        name="build",
    )(*operands)
    return list(outs[:-1]), outs[-1]


def apply_body(*refs, tiles, last):
    if last:
        me_ref, refs = refs[0], refs[1:]
    vector_ref, tile_refs, refs = refs[0], refs[1 : 1 + tiles], refs[1 + tiles :]
    out_ref, flat_ref = refs[-2:]
    blocks, _, size = vector_ref.shape
    for n in range(blocks):
        flat_ref[:, n * size : (n + 1) * size] = vector_ref[n]
    place = 0
    for tile_ref in tile_refs:
        product = jnp.dot(flat_ref[...], tile_ref[...], preferred_element_type=F32)
        for n in range(product.shape[1] // size):
            value = product[:, n * size : (n + 1) * size]
            if last:
                out_ref[place ^ me_ref[0]] = (value + refs[0][place]).astype(out_ref.dtype)
            else:
                out_ref[place] = value
            place += 1


def apply(vector, tiles, carried, me):
    blocks, vectors, size = vector.shape
    points, wide = tiles[0].shape
    last = carried is not None
    operands = [vector] + tiles
    in_specs = [VMEM] * len(operands)
    if last:
        operands = [me] + operands + [carried]
        in_specs = [SMEM] + in_specs + [VMEM]
    total = len(tiles) * wide
    return pl.pallas_call(
        functools.partial(apply_body, tiles=len(tiles), last=last),
        in_specs=in_specs,
        out_specs=VMEM,
        out_shape=pltpu.VMEM((total // size, vectors, size), BF16 if last else F32),
        scratch_shapes=[pltpu.VMEM((vectors, points), BF16)],
        compiler_params=pltpu.CompilerParams(vmem_limit_bytes=4 << 20),
        cost_estimate=pl.CostEstimate(
            flops=2 * points * total * 256,
            bytes_accessed=2 * points * total,
            transcendentals=0,
        ),
        name="apply",
    )(*operands)


def first_body(received_ref, targets_ref, start_ref, residual_ref, line_ref):
    product = jnp.sum(received_ref[...].astype(F32), axis=0)
    residual = targets_ref[...] - (start_ref[...] + product)
    residual_ref[...] = residual
    rounded = residual.astype(BF16)
    for n in range(line_ref.shape[0]):
        line_ref[n] = rounded


def sums_body(received_ref, residual_ref, product_ref, sums_ref):
    product = jnp.sum(received_ref[...].astype(F32), axis=0)
    product_ref[...] = product
    residual = residual_ref[...]
    vectors = residual.shape[0]
    one = jnp.sum(residual * residual, axis=1, keepdims=True)
    two = jnp.sum(residual * product, axis=1, keepdims=True)
    three = jnp.sum(product * product, axis=1, keepdims=True)
    lane = lax.broadcasted_iota(jnp.int32, (vectors, 128), 1)
    table = jnp.where(lane == 0, one, jnp.where(lane == 1, two, jnp.where(lane == 2, three, 0.0)))
    table = jnp.concatenate([table, jnp.zeros((128 - vectors, 128), F32)], axis=0).T[0:8, :]
    for n in range(sums_ref.shape[0]):
        sums_ref[n] = table


def spread_body(received_ref, sums_ref):
    table = jnp.sum(received_ref[...], axis=0)
    for n in range(sums_ref.shape[0]):
        sums_ref[n] = table


def last_body(
    received_ref, start_ref, residual_ref, product_ref, solution_ref, new_ref, direction_ref
):
    vectors = start_ref.shape[0]
    table = jnp.sum(received_ref[...], axis=0)
    table = jnp.concatenate([table, jnp.zeros((120, 128), F32)], axis=0).T[0:vectors, :]
    one, two, three = table[:, 0:1], table[:, 1:2], table[:, 2:3]
    alpha = one / (one + two)
    norm_new = alpha * alpha * jnp.maximum(three - two * two / one, 0.0)
    residual = residual_ref[...]
    image = residual + product_ref[...]
    solution_ref[...] = start_ref[...] + alpha * residual
    new = residual - alpha * image
    new_ref[...] = new
    direction_ref[...] = new + (norm_new / one) * residual


def small(body, name, outs, operands):
    return pl.pallas_call(
        body,
        in_specs=[SMEM if operand.size == 1 else VMEM for operand in operands],
        out_specs=[VMEM] * len(outs),
        out_shape=outs,
        compiler_params=pltpu.CompilerParams(vmem_limit_bytes=4 << 20),
        name=name,
    )(*operands)


def per_device(features, groups, targets, start):
    width, size = features.shape
    vectors = start.shape[0]
    planes = lax.axis_size(PLANE)
    lines = lax.axis_size(LINE)
    scale = scale_of(width)
    amplitude = AMP_NUM / math.sqrt(size * planes * lines * lax.axis_size("core"))
    gain = -math.log2(RHO) / scale
    gains = constant_pieces(gain)
    shift = 0.5 * (math.log2(amplitude) / scale - gain)

    me = lax.axis_index(PLANE).astype(jnp.int32).reshape(1)

    def across(value, axis, step=1):
        count = lax.axis_size(axis)
        return lax.ppermute(value, axis, [(n, n ^ step) for n in range(count)])

    own, line = pl.pallas_call(
        functools.partial(pack_body, shift=shift),
        in_specs=[HBM] * 3,
        out_shape=[
            jax.ShapeDtypeStruct((1, HEAD, size), BF16),
            jax.ShapeDtypeStruct((lines, HEAD + vectors, size), BF16),
        ],
        scratch_shapes=[
            pltpu.VMEM((width, size), BF16),
            pltpu.VMEM((1, size), jnp.int32),
            pltpu.VMEM((vectors, size), F32),
            pltpu.SemaphoreType.DMA((3,)),
        ],
        name="pack",
    )(features, groups.reshape(1, size), start)
    line = lax.all_to_all(line, LINE, 0, 0)
    side = [own] + [across(own, ("yl", "yh"), step) for step in (1, 2, 3)]
    side = jnp.concatenate(side, axis=0)
    parts = [side, across(side, "x", 1)]

    def right_of(part):
        (out,) = small(
            functools.partial(right_body, gains),
            "right",
            [pltpu.VMEM((DEPTH, part.shape[0] * size), BF16)],
            [part],
        )
        return out

    def left_of(value):
        points = value.shape[0] * size
        return small(
            left_body,
            "left",
            [pltpu.VMEM((points, DEPTH), BF16), pltpu.VMEM((vectors, points), BF16)],
            [me, value],
        )

    rights = [right_of(parts[0])]
    side, rights[0] = lax.optimization_barrier((side, rights[0]))
    parts.append(across(side, "x", 2))
    line, rights[0] = lax.optimization_barrier((line, rights[0]))
    near = across(line, "core")
    left, vector = left_of(line)
    tiles, carried = [None] * 4, [None] * 4
    for n in range(3):
        if n > 0:
            left, part = lax.optimization_barrier((left, parts[n]))
            rights.append(right_of(part))
        if n == 2:
            parts.append(across(part, "x", 1))
        (tiles[n],), carried[n] = build(left, vector, rights[n:], [], size, scale, me)
        left, carried[n] = lax.optimization_barrier((left, carried[n]))
    near, carried[2] = lax.optimization_barrier((near, carried[2]))
    near_left, near_vector = left_of(near)
    near_tiles, done = build(near_left, near_vector, rights, carried[:3], size, scale, me)
    left, part, done = lax.optimization_barrier((left, parts[3], done))
    rights.append(right_of(part))
    tiles[3:], carried[3] = build(left, vector, rights[3:], [], size, scale, me)
    last_tile, partial_value = build(
        near_left, near_vector, rights[3:], [done, carried[3]], size, scale, me, last=True
    )
    near_tiles = near_tiles + last_tile
    received = lax.all_to_all(partial_value, PLANE, 0, 0)

    residual0, vector = small(
        first_body,
        "first",
        [pltpu.VMEM((vectors, size), F32), pltpu.VMEM((lines, vectors, size), BF16)],
        [received, targets, start],
    )
    vector = lax.all_to_all(vector, LINE, 0, 0)
    near = across(vector, "core")
    total = apply(vector, tiles, None, me)
    partial_value = apply(near, near_tiles, total, me)
    received = lax.all_to_all(partial_value, PLANE, 0, 0)

    product, sums = small(
        sums_body,
        "sums",
        [pltpu.VMEM((vectors, size), F32), pltpu.VMEM((8, 8, 128), F32)],
        [received, residual0],
    )
    sums = lax.all_to_all(sums, ('x', 'core'), 0, 0)
    (sums,) = small(spread_body, "spread", [pltpu.VMEM((32, 8, 128), F32)], [sums])
    sums = lax.all_to_all(sums, ('yl', 'yh', 'z'), 0, 0)
    return tuple(
        small(
            last_body,
            "last",
            [jax.ShapeDtypeStruct((vectors, size), F32)] * 3,
            [sums, start, residual0, product],
        )
    )


def solution(mesh):
    fine = Mesh(mesh.devices.reshape(2, 4, 2, 8, 2), AXES)
    split = ("yh", "z", "core", "yl", "x")
    in_specs = (P(None, split), P(split), P(None, split), P(None, split))
    out_specs = (P(None, split),) * 3
    return jax.shard_map(
        per_device, mesh=fine, in_specs=in_specs, out_specs=out_specs, check_vma=False
    )
```

```python
import functools
import math

import jax
import jax.numpy as jnp
from jax import lax
from jax.experimental import pallas as pl
from jax.experimental.pallas import tpu as pltpu
from jax.sharding import Mesh, PartitionSpec as P

RHO = 0.2
AMP_NUM = 16.0

AXES = ("yl", "x", "yh", "z", "core")
PLANE = ("x", "yh", "yl")
LINE = ("z",)

BF16 = jnp.bfloat16
F32 = jnp.float32
VMEM = pl.BlockSpec(memory_space=pltpu.VMEM)
SMEM = pl.BlockSpec(memory_space=pltpu.SMEM)
HBM = pl.BlockSpec(memory_space=pltpu.HBM)

HEAD = 80
DEPTH = 128


def scale_of(width):
    return 2.0 * math.log2(math.e) / width


def pieces_of(value):
    first = value.astype(BF16).astype(F32)
    rest = value - first
    second = rest.astype(BF16).astype(F32)
    return first, second, rest - second


def constant_pieces(value):
    import numpy as np
    import ml_dtypes

    out = []
    rest = value
    for _ in range(3):
        piece = float(np.float32(rest).astype(ml_dtypes.bfloat16))
        out.append(piece)
        rest = rest - piece
    return out


def pack_body(
    features_hbm, groups_hbm, start_hbm, own_ref, line_ref, features_ref, groups_ref, start_ref, sems,
    *, shift
):
    copies = [
        pltpu.make_async_copy(source, target, sems.at[n])
        for n, (source, target) in enumerate(
            ((features_hbm, features_ref), (groups_hbm, groups_ref), (start_hbm, start_ref))
        )
    ]
    for copy in copies:
        copy.start()
    for copy in copies:
        copy.wait()
    features = features_ref[...]
    wide = features.astype(F32)
    half = shift - 0.5 * jnp.sum(wide * wide, axis=0, keepdims=True)
    first, second, third = pieces_of(half)
    group = groups_ref[...].astype(F32)
    count = features.shape[1]
    row = lax.broadcasted_iota(jnp.int32, (16, count), 0)
    tail = jnp.where(row == 0, first, 0.0)
    tail = jnp.where(row == 1, second, tail)
    tail = jnp.where(row == 2, third, tail)
    tail = jnp.where(row == 3, group, tail).astype(BF16)
    vector = start_ref[...].astype(BF16)
    own_ref[0, 0:64, :] = features
    own_ref[0, 64:80, :] = tail
    for n in range(line_ref.shape[0]):
        line_ref[n, 0:64, :] = features
        line_ref[n, 64:80, :] = tail
        line_ref[n, 80:112, :] = vector


def tail_rows(packed, left, gains):
    count = packed.shape[1]
    head = packed.astype(F32)
    first, second, third, group = (head[n : n + 1, :] for n in range(4))
    row = lax.broadcasted_iota(jnp.int32, (64, count), 0)
    level = (row & 7).astype(F32)
    hot = jnp.where(level == group, 1.0, 0.0)
    if not left:
        hot = hot * jnp.where(row < 16, gains[0], jnp.where(row < 24, gains[1], gains[2]))
    out = jnp.where((row >= 8) & (row < 32), hot, 0.0)
    base = 0 if left else 3
    out = jnp.where((row >= 3 - base) & (row < 6 - base), 1.0, out)
    out = jnp.where(row == base, first, out)
    out = jnp.where(row == base + 1, second, out)
    out = jnp.where(row == base + 2, third, out)
    return out.astype(BF16)


def right_body(gains, block_ref, right_ref):
    size = block_ref.shape[2]
    for n in range(block_ref.shape[0]):
        columns = slice(n * size, (n + 1) * size)
        right_ref[0:64, columns] = block_ref[n, 0:64, :]
        right_ref[64:128, columns] = tail_rows(block_ref[n, 64:80, :], False, gains)


def left_body(me_ref, line_ref, left_ref, vector_ref):
    blocks, _, size = line_ref.shape
    for n in range(blocks):
        rows = line_ref[n, 0:64, :]
        tail = tail_rows(line_ref[n, 64:80, :], True, None)
        left_ref[n * size : (n + 1) * size, :] = jnp.concatenate([rows, tail], axis=0).T
        vector_ref[:, n * size : (n + 1) * size] = line_ref[n, 80:112, :]


def build_body(scale, *refs, groups, last):
    if last:
        me_ref, refs = refs[0], refs[1:]
    left_ref, vector_ref, right_refs, refs = refs[0], refs[1], refs[2 : 2 + groups], refs[2 + groups :]
    carried_refs, tile_refs, out_ref = refs[: -groups - 1], refs[-groups - 1 : -1], refs[-1]
    points = left_ref.shape[0]
    size = out_ref.shape[2]
    place = 0

    def put(value):
        if last:
            out_ref[place ^ me_ref[0]] = value.astype(out_ref.dtype)
        else:
            out_ref[place] = value

    if last:
        for n in range(carried_refs[0].shape[0]):
            put(carried_refs[0][n])
            place += 1
        carried_refs = carried_refs[1:]
    for group in range(groups):
        right = right_refs[group][...]
        tile_ref = tile_refs[group]
        for n in range(0, points, 256):
            power = jnp.dot(left_ref[n : n + 256, :], right, preferred_element_type=F32)
            tile_ref[n : n + 256, :] = jnp.exp2(power * scale).astype(BF16)
        product = jnp.dot(vector_ref[...], tile_ref[...], preferred_element_type=F32)
        for n in range(product.shape[1] // size):
            value = product[:, n * size : (n + 1) * size]
            if carried_refs:
                value = value + carried_refs[group][n]
            put(value)
            place += 1


def build(left, vector, rights, carried, size, scale, me, last=False):
    points, wide = left.shape[0], rights[0].shape[1]
    vectors = vector.shape[0]
    operands = [left, vector] + rights + carried
    in_specs = [VMEM] * len(operands)
    if last:
        operands = [me] + operands
        in_specs = [SMEM] + in_specs
    total = len(rights) * wide
    blocks = total // size + (carried[0].shape[0] if last else 0)
    outs = pl.pallas_call(
        functools.partial(build_body, scale, groups=len(rights), last=last),
        in_specs=in_specs,
        out_specs=[VMEM] * (len(rights) + 1),
        out_shape=[pltpu.VMEM((points, wide), BF16)] * len(rights)
        + [pltpu.VMEM((blocks, vectors, size), BF16 if last else F32)],
        compiler_params=pltpu.CompilerParams(vmem_limit_bytes=8 << 20),
        cost_estimate=pl.CostEstimate(
            flops=2 * points * total * 512,
            bytes_accessed=2 * points * total,
            transcendentals=points * total,
        ),
        name="build",
    )(*operands)
    return list(outs[:-1]), outs[-1]


def apply_body(*refs, tiles, last):
    if last:
        me_ref, refs = refs[0], refs[1:]
    vector_ref, tile_refs, refs = refs[0], refs[1 : 1 + tiles], refs[1 + tiles :]
    out_ref, flat_ref = refs[-2:]
    blocks, _, size = vector_ref.shape
    for n in range(blocks):
        flat_ref[:, n * size : (n + 1) * size] = vector_ref[n]
    place = 0
    for tile_ref in tile_refs:
        product = jnp.dot(flat_ref[...], tile_ref[...], preferred_element_type=F32)
        for n in range(product.shape[1] // size):
            value = product[:, n * size : (n + 1) * size]
            if last:
                out_ref[place ^ me_ref[0]] = (value + refs[0][place]).astype(out_ref.dtype)
            else:
                out_ref[place] = value
            place += 1


def apply(vector, tiles, carried, me):
    blocks, vectors, size = vector.shape
    points, wide = tiles[0].shape
    last = carried is not None
    operands = [vector] + tiles
    in_specs = [VMEM] * len(operands)
    if last:
        operands = [me] + operands + [carried]
        in_specs = [SMEM] + in_specs + [VMEM]
    total = len(tiles) * wide
    return pl.pallas_call(
        functools.partial(apply_body, tiles=len(tiles), last=last),
        in_specs=in_specs,
        out_specs=VMEM,
        out_shape=pltpu.VMEM((total // size, vectors, size), BF16 if last else F32),
        scratch_shapes=[pltpu.VMEM((vectors, points), BF16)],
        compiler_params=pltpu.CompilerParams(vmem_limit_bytes=4 << 20),
        cost_estimate=pl.CostEstimate(
            flops=2 * points * total * 256,
            bytes_accessed=2 * points * total,
            transcendentals=0,
        ),
        name="apply",
    )(*operands)


def first_body(received_ref, targets_ref, start_ref, residual_ref, line_ref):
    product = jnp.sum(received_ref[...].astype(F32), axis=0)
    residual = targets_ref[...] - (start_ref[...] + product)
    residual_ref[...] = residual
    rounded = residual.astype(BF16)
    for n in range(line_ref.shape[0]):
        line_ref[n] = rounded


def sums_body(received_ref, residual_ref, product_ref, sums_ref):
    product = jnp.sum(received_ref[...].astype(F32), axis=0)
    product_ref[...] = product
    residual = residual_ref[...]
    vectors = residual.shape[0]
    one = jnp.sum(residual * residual, axis=1, keepdims=True)
    two = jnp.sum(residual * product, axis=1, keepdims=True)
    three = jnp.sum(product * product, axis=1, keepdims=True)
    lane = lax.broadcasted_iota(jnp.int32, (vectors, 128), 1)
    table = jnp.where(lane == 0, one, jnp.where(lane == 1, two, jnp.where(lane == 2, three, 0.0)))
    table = jnp.concatenate([table, jnp.zeros((128 - vectors, 128), F32)], axis=0).T[0:8, :]
    for n in range(sums_ref.shape[0]):
        sums_ref[n] = table


def spread_body(received_ref, sums_ref):
    table = jnp.sum(received_ref[...], axis=0)
    for n in range(sums_ref.shape[0]):
        sums_ref[n] = table


def last_body(
    received_ref, start_ref, residual_ref, product_ref, solution_ref, new_ref, direction_ref
):
    vectors = start_ref.shape[0]
    table = jnp.sum(received_ref[...], axis=0)
    table = jnp.concatenate([table, jnp.zeros((120, 128), F32)], axis=0).T[0:vectors, :]
    one, two, three = table[:, 0:1], table[:, 1:2], table[:, 2:3]
    alpha = one / (one + two)
    norm_new = alpha * alpha * jnp.maximum(three - two * two / one, 0.0)
    residual = residual_ref[...]
    image = residual + product_ref[...]
    solution_ref[...] = start_ref[...] + alpha * residual
    new = residual - alpha * image
    new_ref[...] = new
    direction_ref[...] = new + (norm_new / one) * residual


def small(body, name, outs, operands):
    return pl.pallas_call(
        body,
        in_specs=[SMEM if operand.size == 1 else VMEM for operand in operands],
        out_specs=[VMEM] * len(outs),
        out_shape=outs,
        compiler_params=pltpu.CompilerParams(vmem_limit_bytes=4 << 20),
        name=name,
    )(*operands)


def per_device(features, groups, targets, start):
    width, size = features.shape
    vectors = start.shape[0]
    planes = lax.axis_size(PLANE)
    lines = lax.axis_size(LINE)
    scale = scale_of(width)
    amplitude = AMP_NUM / math.sqrt(size * planes * lines * lax.axis_size("core"))
    gain = -math.log2(RHO) / scale
    gains = constant_pieces(gain)
    shift = 0.5 * (math.log2(amplitude) / scale - gain)

    me = lax.axis_index(PLANE).astype(jnp.int32).reshape(1)

    def across(value, axis, step=1):
        count = lax.axis_size(axis)
        return lax.ppermute(value, axis, [(n, n ^ step) for n in range(count)])

    own, line = pl.pallas_call(
        functools.partial(pack_body, shift=shift),
        in_specs=[HBM] * 3,
        out_shape=[
            jax.ShapeDtypeStruct((1, HEAD, size), BF16),
            jax.ShapeDtypeStruct((lines, HEAD + vectors, size), BF16),
        ],
        scratch_shapes=[
            pltpu.VMEM((width, size), BF16),
            pltpu.VMEM((1, size), jnp.int32),
            pltpu.VMEM((vectors, size), F32),
            pltpu.SemaphoreType.DMA((3,)),
        ],
        name="pack",
    )(features, groups.reshape(1, size), start)
    line = lax.all_to_all(line, LINE, 0, 0)
    side = [own] + [across(own, ("yl", "yh"), step) for step in (2, 1, 3)]
    side = jnp.concatenate(side, axis=0)
    parts = [side, across(side, "x", 1)]

    def right_of(part):
        (out,) = small(
            functools.partial(right_body, gains),
            "right",
            [pltpu.VMEM((DEPTH, part.shape[0] * size), BF16)],
            [part],
        )
        return out

    def left_of(value):
        points = value.shape[0] * size
        return small(
            left_body,
            "left",
            [pltpu.VMEM((points, DEPTH), BF16), pltpu.VMEM((vectors, points), BF16)],
            [me, value],
        )

    rights = [right_of(parts[0])]
    side, rights[0] = lax.optimization_barrier((side, rights[0]))
    parts.append(across(side, "x", 2))
    line, rights[0] = lax.optimization_barrier((line, rights[0]))
    near = across(line, "core")
    left, vector = left_of(line)
    tiles, carried = [None] * 4, [None] * 4
    for n in range(3):
        if n > 0:
            left, part = lax.optimization_barrier((left, parts[n]))
            rights.append(right_of(part))
        if n == 2:
            parts.append(across(part, "x", 1))
        (tiles[n],), carried[n] = build(left, vector, rights[n:], [], size, scale, me)
        left, carried[n] = lax.optimization_barrier((left, carried[n]))
    near, carried[2] = lax.optimization_barrier((near, carried[2]))
    near_left, near_vector = left_of(near)
    near_tiles, done = build(near_left, near_vector, rights, carried[:3], size, scale, me)
    left, part, done = lax.optimization_barrier((left, parts[3], done))
    rights.append(right_of(part))
    tiles[3:], carried[3] = build(left, vector, rights[3:], [], size, scale, me)
    last_tile, partial_value = build(
        near_left, near_vector, rights[3:], [done, carried[3]], size, scale, me, last=True
    )
    near_tiles = near_tiles + last_tile
    received = lax.all_to_all(partial_value, PLANE, 0, 0)

    residual0, vector = small(
        first_body,
        "first",
        [pltpu.VMEM((vectors, size), F32), pltpu.VMEM((lines, vectors, size), BF16)],
        [received, targets, start],
    )
    vector = lax.all_to_all(vector, LINE, 0, 0)
    near = across(vector, "core")
    total = apply(vector, tiles, None, me)
    partial_value = apply(near, near_tiles, total, me)
    received = lax.all_to_all(partial_value, PLANE, 0, 0)

    product, sums = small(
        sums_body,
        "sums",
        [pltpu.VMEM((vectors, size), F32), pltpu.VMEM((8, 8, 128), F32)],
        [received, residual0],
    )
    sums = lax.all_to_all(sums, ('x', 'core'), 0, 0)
    (sums,) = small(spread_body, "spread", [pltpu.VMEM((32, 8, 128), F32)], [sums])
    sums = lax.all_to_all(sums, ('yh', 'yl', 'z'), 0, 0)
    return tuple(
        small(
            last_body,
            "last",
            [jax.ShapeDtypeStruct((vectors, size), F32)] * 3,
            [sums, start, residual0, product],
        )
    )


def solution(mesh):
    fine = Mesh(mesh.devices.reshape(2, 4, 2, 8, 2), AXES)
    split = ("yh", "z", "core", "yl", "x")
    in_specs = (P(None, split), P(split), P(None, split), P(None, split))
    out_specs = (P(None, split),) * 3
    return jax.shard_map(
        per_device, mesh=fine, in_specs=in_specs, out_specs=out_specs, check_vma=False
    )
```

```python
import functools
import math

import jax
import jax.numpy as jnp
from jax import lax
from jax.experimental import pallas as pl
from jax.experimental.pallas import tpu as pltpu
from jax.sharding import Mesh, PartitionSpec as P

RHO = 0.2
AMP_NUM = 16.0

AXES = ("yl", "x", "yh", "z", "core")
PLANE = ("x", "yl", "yh")
LINE = ("z",)

BF16 = jnp.bfloat16
F32 = jnp.float32
VMEM = pl.BlockSpec(memory_space=pltpu.VMEM)
SMEM = pl.BlockSpec(memory_space=pltpu.SMEM)
HBM = pl.BlockSpec(memory_space=pltpu.HBM)

HEAD = 80
DEPTH = 128


def scale_of(width):
    return 2.0 * math.log2(math.e) / width


def pieces_of(value):
    first = value.astype(BF16).astype(F32)
    rest = value - first
    second = rest.astype(BF16).astype(F32)
    return first, second, rest - second


def constant_pieces(value):
    import numpy as np
    import ml_dtypes

    out = []
    rest = value
    for _ in range(3):
        piece = float(np.float32(rest).astype(ml_dtypes.bfloat16))
        out.append(piece)
        rest = rest - piece
    return out


def pack_body(
    features_hbm, groups_hbm, start_hbm, own_ref, line_ref, features_ref, groups_ref, start_ref, sems,
    *, shift
):
    copies = [
        pltpu.make_async_copy(source, target, sems.at[n])
        for n, (source, target) in enumerate(
            ((features_hbm, features_ref), (groups_hbm, groups_ref), (start_hbm, start_ref))
        )
    ]
    for copy in copies:
        copy.start()
    for copy in copies:
        copy.wait()
    features = features_ref[...]
    wide = features.astype(F32)
    half = shift - 0.5 * jnp.sum(wide * wide, axis=0, keepdims=True)
    first, second, third = pieces_of(half)
    group = groups_ref[...].astype(F32)
    count = features.shape[1]
    row = lax.broadcasted_iota(jnp.int32, (16, count), 0)
    tail = jnp.where(row == 0, first, 0.0)
    tail = jnp.where(row == 1, second, tail)
    tail = jnp.where(row == 2, third, tail)
    tail = jnp.where(row == 3, group, tail).astype(BF16)
    vector = start_ref[...].astype(BF16)
    own_ref[0, 0:64, :] = features
    own_ref[0, 64:80, :] = tail
    for n in range(line_ref.shape[0]):
        line_ref[n, 0:64, :] = features
        line_ref[n, 64:80, :] = tail
        line_ref[n, 80:112, :] = vector


def tail_rows(packed, left, gains):
    count = packed.shape[1]
    head = packed.astype(F32)
    first, second, third, group = (head[n : n + 1, :] for n in range(4))
    row = lax.broadcasted_iota(jnp.int32, (64, count), 0)
    level = (row & 7).astype(F32)
    hot = jnp.where(level == group, 1.0, 0.0)
    if not left:
        hot = hot * jnp.where(row < 16, gains[0], jnp.where(row < 24, gains[1], gains[2]))
    out = jnp.where((row >= 8) & (row < 32), hot, 0.0)
    base = 0 if left else 3
    out = jnp.where((row >= 3 - base) & (row < 6 - base), 1.0, out)
    out = jnp.where(row == base, first, out)
    out = jnp.where(row == base + 1, second, out)
    out = jnp.where(row == base + 2, third, out)
    return out.astype(BF16)


def right_body(gains, block_ref, right_ref):
    size = block_ref.shape[2]
    for n in range(block_ref.shape[0]):
        columns = slice(n * size, (n + 1) * size)
        right_ref[0:64, columns] = block_ref[n, 0:64, :]
        right_ref[64:128, columns] = tail_rows(block_ref[n, 64:80, :], False, gains)


def left_body(me_ref, line_ref, left_ref, vector_ref):
    blocks, _, size = line_ref.shape
    for n in range(blocks):
        rows = line_ref[n, 0:64, :]
        tail = tail_rows(line_ref[n, 64:80, :], True, None)
        left_ref[n * size : (n + 1) * size, :] = jnp.concatenate([rows, tail], axis=0).T
        vector_ref[:, n * size : (n + 1) * size] = line_ref[n, 80:112, :]


def build_body(scale, *refs, groups, last):
    if last:
        me_ref, refs = refs[0], refs[1:]
    left_ref, vector_ref, right_refs, refs = refs[0], refs[1], refs[2 : 2 + groups], refs[2 + groups :]
    carried_refs, tile_refs, out_ref = refs[: -groups - 1], refs[-groups - 1 : -1], refs[-1]
    points = left_ref.shape[0]
    size = out_ref.shape[2]
    place = 0

    def put(value):
        if last:
            out_ref[place ^ me_ref[0]] = value.astype(out_ref.dtype)
        else:
            out_ref[place] = value

    if last:
        for n in range(carried_refs[0].shape[0]):
            put(carried_refs[0][n])
            place += 1
        carried_refs = carried_refs[1:]
    for group in range(groups):
        right = right_refs[group][...]
        tile_ref = tile_refs[group]
        for n in range(0, points, 256):
            power = jnp.dot(left_ref[n : n + 256, :], right, preferred_element_type=F32)
            tile_ref[n : n + 256, :] = jnp.exp2(power * scale).astype(BF16)
        product = jnp.dot(vector_ref[...], tile_ref[...], preferred_element_type=F32)
        for n in range(product.shape[1] // size):
            value = product[:, n * size : (n + 1) * size]
            if carried_refs:
                value = value + carried_refs[group][n]
            put(value)
            place += 1


def build(left, vector, rights, carried, size, scale, me, last=False):
    points, wide = left.shape[0], rights[0].shape[1]
    vectors = vector.shape[0]
    operands = [left, vector] + rights + carried
    in_specs = [VMEM] * len(operands)
    if last:
        operands = [me] + operands
        in_specs = [SMEM] + in_specs
    total = len(rights) * wide
    blocks = total // size + (carried[0].shape[0] if last else 0)
    outs = pl.pallas_call(
        functools.partial(build_body, scale, groups=len(rights), last=last),
        in_specs=in_specs,
        out_specs=[VMEM] * (len(rights) + 1),
        out_shape=[pltpu.VMEM((points, wide), BF16)] * len(rights)
        + [pltpu.VMEM((blocks, vectors, size), BF16 if last else F32)],
        compiler_params=pltpu.CompilerParams(vmem_limit_bytes=8 << 20),
        cost_estimate=pl.CostEstimate(
            flops=2 * points * total * 512,
            bytes_accessed=2 * points * total,
            transcendentals=points * total,
        ),
        name="build",
    )(*operands)
    return list(outs[:-1]), outs[-1]


def apply_body(*refs, tiles, last):
    if last:
        me_ref, refs = refs[0], refs[1:]
    vector_ref, tile_refs, refs = refs[0], refs[1 : 1 + tiles], refs[1 + tiles :]
    out_ref, flat_ref = refs[-2:]
    blocks, _, size = vector_ref.shape
    for n in range(blocks):
        flat_ref[:, n * size : (n + 1) * size] = vector_ref[n]
    place = 0
    for tile_ref in tile_refs:
        product = jnp.dot(flat_ref[...], tile_ref[...], preferred_element_type=F32)
        for n in range(product.shape[1] // size):
            value = product[:, n * size : (n + 1) * size]
            if last:
                out_ref[place ^ me_ref[0]] = (value + refs[0][place]).astype(out_ref.dtype)
            else:
                out_ref[place] = value
            place += 1


def apply(vector, tiles, carried, me):
    blocks, vectors, size = vector.shape
    points, wide = tiles[0].shape
    last = carried is not None
    operands = [vector] + tiles
    in_specs = [VMEM] * len(operands)
    if last:
        operands = [me] + operands + [carried]
        in_specs = [SMEM] + in_specs + [VMEM]
    total = len(tiles) * wide
    return pl.pallas_call(
        functools.partial(apply_body, tiles=len(tiles), last=last),
        in_specs=in_specs,
        out_specs=VMEM,
        out_shape=pltpu.VMEM((total // size, vectors, size), BF16 if last else F32),
        scratch_shapes=[pltpu.VMEM((vectors, points), BF16)],
        compiler_params=pltpu.CompilerParams(vmem_limit_bytes=4 << 20),
        cost_estimate=pl.CostEstimate(
            flops=2 * points * total * 256,
            bytes_accessed=2 * points * total,
            transcendentals=0,
        ),
        name="apply",
    )(*operands)


def first_body(received_ref, targets_ref, start_ref, residual_ref, line_ref):
    product = jnp.sum(received_ref[...].astype(F32), axis=0)
    residual = targets_ref[...] - (start_ref[...] + product)
    residual_ref[...] = residual
    rounded = residual.astype(BF16)
    for n in range(line_ref.shape[0]):
        line_ref[n] = rounded


def sums_body(received_ref, residual_ref, product_ref, sums_ref):
    product = jnp.sum(received_ref[...].astype(F32), axis=0)
    product_ref[...] = product
    residual = residual_ref[...]
    vectors = residual.shape[0]
    one = jnp.sum(residual * residual, axis=1, keepdims=True)
    two = jnp.sum(residual * product, axis=1, keepdims=True)
    three = jnp.sum(product * product, axis=1, keepdims=True)
    lane = lax.broadcasted_iota(jnp.int32, (vectors, 128), 1)
    table = jnp.where(lane == 0, one, jnp.where(lane == 1, two, jnp.where(lane == 2, three, 0.0)))
    table = jnp.concatenate([table, jnp.zeros((128 - vectors, 128), F32)], axis=0).T[0:8, :]
    for n in range(sums_ref.shape[0]):
        sums_ref[n] = table


def spread_body(received_ref, sums_ref):
    table = jnp.sum(received_ref[...], axis=0)
    for n in range(sums_ref.shape[0]):
        sums_ref[n] = table


def last_body(
    received_ref, start_ref, residual_ref, product_ref, solution_ref, new_ref, direction_ref
):
    vectors = start_ref.shape[0]
    table = jnp.sum(received_ref[...], axis=0)
    table = jnp.concatenate([table, jnp.zeros((120, 128), F32)], axis=0).T[0:vectors, :]
    one, two, three = table[:, 0:1], table[:, 1:2], table[:, 2:3]
    alpha = one / (one + two)
    norm_new = alpha * alpha * jnp.maximum(three - two * two / one, 0.0)
    residual = residual_ref[...]
    image = residual + product_ref[...]
    solution_ref[...] = start_ref[...] + alpha * residual
    new = residual - alpha * image
    new_ref[...] = new
    direction_ref[...] = new + (norm_new / one) * residual


def small(body, name, outs, operands):
    return pl.pallas_call(
        body,
        in_specs=[SMEM if operand.size == 1 else VMEM for operand in operands],
        out_specs=[VMEM] * len(outs),
        out_shape=outs,
        compiler_params=pltpu.CompilerParams(vmem_limit_bytes=4 << 20),
        name=name,
    )(*operands)


def per_device(features, groups, targets, start):
    width, size = features.shape
    vectors = start.shape[0]
    planes = lax.axis_size(PLANE)
    lines = lax.axis_size(LINE)
    scale = scale_of(width)
    amplitude = AMP_NUM / math.sqrt(size * planes * lines * lax.axis_size("core"))
    gain = -math.log2(RHO) / scale
    gains = constant_pieces(gain)
    shift = 0.5 * (math.log2(amplitude) / scale - gain)

    me = lax.axis_index(PLANE).astype(jnp.int32).reshape(1)

    def across(value, axis, step=1):
        count = lax.axis_size(axis)
        return lax.ppermute(value, axis, [(n, n ^ step) for n in range(count)])

    own, line = pl.pallas_call(
        functools.partial(pack_body, shift=shift),
        in_specs=[HBM] * 3,
        out_shape=[
            jax.ShapeDtypeStruct((1, HEAD, size), BF16),
            jax.ShapeDtypeStruct((lines, HEAD + vectors, size), BF16),
        ],
        scratch_shapes=[
            pltpu.VMEM((width, size), BF16),
            pltpu.VMEM((1, size), jnp.int32),
            pltpu.VMEM((vectors, size), F32),
            pltpu.SemaphoreType.DMA((3,)),
        ],
        name="pack",
    )(features, groups.reshape(1, size), start)
    line = lax.all_to_all(line, LINE, 0, 0)
    side = [own] + [across(own, ("yl", "yh"), step) for step in (1, 2, 3)]
    side = jnp.concatenate(side, axis=0)
    parts = [side, across(side, "x", 1)]

    def right_of(part):
        (out,) = small(
            functools.partial(right_body, gains),
            "right",
            [pltpu.VMEM((DEPTH, part.shape[0] * size), BF16)],
            [part],
        )
        return out

    def left_of(value):
        points = value.shape[0] * size
        return small(
            left_body,
            "left",
            [pltpu.VMEM((points, DEPTH), BF16), pltpu.VMEM((vectors, points), BF16)],
            [me, value],
        )

    rights = [right_of(parts[0])]
    side, rights[0] = lax.optimization_barrier((side, rights[0]))
    parts.append(across(side, "x", 2))
    line, rights[0] = lax.optimization_barrier((line, rights[0]))
    near = across(line, "core")
    left, vector = left_of(line)
    tiles, carried = [None] * 4, [None] * 4
    for n in range(3):
        if n > 0:
            left, part = lax.optimization_barrier((left, parts[n]))
            rights.append(right_of(part))
        if n == 2:
            parts.append(across(part, "x", 1))
        (tiles[n],), carried[n] = build(left, vector, rights[n:], [], size, scale, me)
        left, carried[n] = lax.optimization_barrier((left, carried[n]))
    near, carried[2] = lax.optimization_barrier((near, carried[2]))
    near_left, near_vector = left_of(near)
    near_tiles, done = build(near_left, near_vector, rights, carried[:3], size, scale, me)
    left, part, done = lax.optimization_barrier((left, parts[3], done))
    rights.append(right_of(part))
    tiles[3:], carried[3] = build(left, vector, rights[3:], [], size, scale, me)
    last_tile, partial_value = build(
        near_left, near_vector, rights[3:], [done, carried[3]], size, scale, me, last=True
    )
    near_tiles = near_tiles + last_tile
    received = lax.all_to_all(partial_value, PLANE, 0, 0)

    residual0, vector = small(
        first_body,
        "first",
        [pltpu.VMEM((vectors, size), F32), pltpu.VMEM((lines, vectors, size), BF16)],
        [received, targets, start],
    )
    vector = lax.all_to_all(vector, LINE, 0, 0)
    near = across(vector, "core")
    total = apply(vector, tiles, None, me)
    partial_value = apply(near, near_tiles, total, me)
    received = lax.all_to_all(partial_value, PLANE, 0, 0)

    product, sums = small(
        sums_body,
        "sums",
        [pltpu.VMEM((vectors, size), F32), pltpu.VMEM((2 * planes, 8, 128), F32)],
        [received, residual0],
    )
    sums = lax.all_to_all(sums, ("yl", "x", "yh", "core"), 0, 0)
    (sums,) = small(spread_body, "spread", [pltpu.VMEM((lines, 8, 128), F32)], [sums])
    sums = lax.all_to_all(sums, LINE, 0, 0)
    return tuple(
        small(
            last_body,
            "last",
            [jax.ShapeDtypeStruct((vectors, size), F32)] * 3,
            [sums, start, residual0, product],
        )
    )


def solution(mesh):
    fine = Mesh(mesh.devices.reshape(2, 4, 2, 8, 2), AXES)
    split = ("yh", "z", "core", "yl", "x")
    in_specs = (P(None, split), P(split), P(None, split), P(None, split))
    out_specs = (P(None, split),) * 3
    return jax.shard_map(
        per_device, mesh=fine, in_specs=in_specs, out_specs=out_specs, check_vma=False
    )
```
